32 devices in a mesh: dp: 4 (over z), expert: 8 (over y, x, core).
Axes of the slice: x: 2, y: 2, z: 4, core: 2. Of those that a mesh axis runs over, the one named last changes fastest.
Arguments:
- tokens: bfloat16 [4096, 1024], P(('dp', 'expert')), may hold values from -6 to 6
- expert_ids: int32 [4096, 8], P(('dp', 'expert')), may hold values from 0 to 15, all different within a row; in each aligned block of 128 rows (0 to 127, 128 to 255, ...) at most 68 rows name the same one
- gate_values: float32 [4096, 8], P(('dp', 'expert')), may hold values from 0.05 to 0.5
- w_gate: bfloat16 [16, 1024, 384], P('expert', 'dp'), may hold values from -0.1875 to 0.1875
- w_up: bfloat16 [16, 1024, 384], P('expert', 'dp'), may hold values from -0.1875 to 0.1875
- w_down: bfloat16 [16, 384, 1024], P('expert', 'dp'), may hold values from -0.3125 to 0.3125
- partner: int32 [32], replicated, may hold values from 0 to 31, as said below
Outputs:
- contrast_loss: float32 [], replicated
- token_grad: bfloat16 [4096, 1024], P(('dp', 'expert'))
- gate_grad: float32 [4096, 8], P(('dp', 'expert'))
The draws below stay inside these ranges and needn't reach their ends.
Inputs may be any that keep to these rules, and one draw needn't show every extreme that they name: `expert_ids`: each row names 8 different experts. Among the 128 rows of one sequence no expert is named more than 68 times, and in every draw some sequence names some expert exactly 68 times. partner[i] differs from i.
All inputs are finite; a program needn't handle non-finite values.
Results may differ from the reference program's by a relative error of at most 0.014.
Values may be sent and summed in bfloat16 or wider, within the bound.
A program may use at most 64 MiB of HBM per device.

```python
import math
import jax
import jax.numpy as jnp
import numpy as np
from jax import lax

D = 1024
FF = 384
TOPK = 8
TOK_DEV = 128
EXPERTS = 16
CAP = 68
BATCH = 32
TOKENS = 4096


def draw_partner(key, part):
    offset = jax.random.randint(key, (BATCH,), 1, BATCH, dtype=jnp.int32)
    return ((jnp.arange(BATCH, dtype=jnp.int32) + offset) % BATCH).astype(jnp.int32)


def steps_of(own_key, shape, cuts, low, largest):
    loudness = 1.0
    for dim, blocks in cuts:
        steps = jax.random.uniform(jax.random.fold_in(jax.random.fold_in(own_key, 6), dim), (blocks,), jnp.float32, low / len(cuts), largest / len(cuts))
        loudness = loudness * jnp.repeat(jnp.exp(steps), shape[dim] // blocks).reshape((-1,) + (1,) * (len(shape) - 1 - dim))
    return loudness


def shared_out(key, own, number, rows, amount, top, bound, lean):
    sequence = jax.random.permutation(key, amount)
    heavy_load, usual = shares(amount, rows * top, bound, lean, True), shares(amount, rows * top, bound, lean, False)
    places = jnp.arange(amount)

    def named(lengths, rotation):
        used = int((lengths > 0).sum())
        fixed = max(1, used // 4)
        moved = fixed + (places - fixed + rotation * (used - fixed)) % max(1, amount - fixed)
        return jnp.zeros((amount,), jnp.int32).at[sequence[jnp.where(places < fixed, places, moved)]].set(jnp.asarray(lengths, jnp.int32))

    lengths = jnp.where(number % 4 == 0, named(heavy_load, number // 4), named(usual, number - number // 4 - 1))
    mixed = jax.random.permutation(jax.random.fold_in(own, 3), amount)
    giver, taker = mixed[0:amount // 2 * 2:2], mixed[1:amount // 2 * 2:2]
    margin = jnp.minimum(lengths[giver] - 1, bound - lengths[taker]) // 2
    margin = jnp.where((giver == sequence[0]) | (taker == sequence[0]) | (lengths[taker] == 0), 0, jnp.maximum(margin, 0))
    moved = jax.random.randint(jax.random.fold_in(own, 4), (amount // 2,), 0, 1 << 20) % (margin + 1)
    lengths = lengths.at[giver].add(-moved).at[taker].add(moved)
    labels = jnp.searchsorted(jnp.cumsum(lengths), jnp.arange(rows * top), side="right").astype(jnp.int32)
    table = labels.reshape(top, rows).T
    table = table[jax.random.permutation(jax.random.fold_in(own, 1), rows)]
    rotation = jax.random.randint(jax.random.fold_in(own, 2), (rows, 1), 0, top)
    return jnp.take_along_axis(table, (jnp.arange(top)[None, :] + rotation) % top, axis=1)


def shares(number_of, total, bound, skew, full):
    weights = [(1 << 20) // math.isqrt(grade ** skew) + 1 for grade in range(1, number_of + 1)]
    largest = bound if full else min(bound, max(-(-total // number_of), total * weights[0] // sum(weights)))
    least = 1 if total - largest >= number_of - 1 else 0
    holding, surplus = [largest] + [least] * (number_of - 1), total - largest - least * (number_of - 1)
    while surplus > 0:
        candidates = [i for i in range(1, number_of) if holding[i] < largest] or [i for i in range(1, number_of) if holding[i] < bound]
        pool, budget = sum([weights[i] for i in candidates]), surplus
        for i in candidates:
            extra = min(bound - holding[i], max(1, budget * weights[i] // pool), surplus)
            holding[i] = holding[i] + extra
            surplus = surplus - extra
    return np.array(holding)


def gaussian(rng, extent, scale, most, pieces=(), held_as=jnp.bfloat16):
    gain = steps_of(rng, extent, pieces, -0.22, 0.18) if pieces else 1.0
    result = jax.random.normal(rng, extent, jnp.float32) * scale * gain
    return jnp.minimum(jnp.maximum(result, -most), most).astype(held_as)


def setup_inputs(seed: int = 0) -> dict:
    key_list = jax.random.split(jax.random.key(seed), 8)
    tokens = gaussian(key_list[0], (TOKENS, D), 1.0, 6.0, ((0, 32),))
    expert_ids_keys = jax.random.split(jax.random.fold_in(key_list[1], 1), TOKENS // TOK_DEV)
    expert_ids_turns = jax.random.permutation(jax.random.fold_in(key_list[1], 3), TOKENS // TOK_DEV)
    expert_ids = jax.vmap(lambda own, number: shared_out(jax.random.fold_in(key_list[1], 2), own, number, TOK_DEV, EXPERTS, TOPK, CAP, 2))(expert_ids_keys, expert_ids_turns).reshape((TOKENS, TOPK))
    gate_values = jnp.clip(jnp.exp(math.log(0.5) - 2.3025851 * jax.random.uniform(key_list[2], (TOKENS, TOPK), jnp.float32) ** steps_of(key_list[2], (TOKENS, TOPK), ((0, 32),), -0.2, 0.2)), 0.05, 0.5)
    w_gate = gaussian(key_list[3], (EXPERTS, D, FF), D ** -0.5, 0.1875, ((0, 8), (1, 4)))
    w_up = gaussian(key_list[4], (EXPERTS, D, FF), D ** -0.5, 0.1875, ((0, 8), (1, 4)))
    w_down = gaussian(key_list[5], (EXPERTS, FF, D), FF ** -0.5, 0.3125, ((0, 8), (1, 4)))
    partner = draw_partner(jax.random.fold_in(key_list[7], 71), 0)
    return dict(tokens=tokens, expert_ids=expert_ids, gate_values=gate_values, w_gate=w_gate, w_up=w_up, w_down=w_down, partner=partner)


score_scale = 20.0
highest = lax.Precision.HIGHEST

def silu_parts(pre_act):
    sigmoid_val = jax.nn.sigmoid(pre_act)
    return (pre_act * sigmoid_val, sigmoid_val * (1.0 + pre_act * (1.0 - sigmoid_val)))

def expert_forward(rows_in, gate_one, up_one, down_one):
    pre_gate = jnp.dot(rows_in, gate_one, preferred_element_type=jnp.float32)
    pre_up = jnp.dot(rows_in, up_one, preferred_element_type=jnp.float32)
    activated, derivative = silu_parts(pre_gate)
    hidden = (activated * pre_up).astype(jnp.bfloat16)
    expert_out = jnp.dot(hidden, down_one, preferred_element_type=jnp.float32).astype(jnp.bfloat16)
    return (pre_gate, pre_up, activated, derivative, expert_out)

def reference(tokens, expert_ids, gate_values, w_gate, w_up, w_down, partner):
    route_ids = expert_ids.reshape(BATCH, TOK_DEV, TOPK)
    gate_rows = gate_values.reshape(BATCH, TOK_DEV, TOPK)
    expert_iota = jnp.arange(EXPERTS, dtype=jnp.int32)
    chosen = lax.optimization_barrier(jnp.sum((route_ids[:, :, :, None] == expert_iota).astype(jnp.int32), axis=2, dtype=jnp.int32))
    before = (jnp.cumsum(chosen, axis=1, dtype=jnp.int32) - chosen).astype(jnp.int32)
    slot_rank = jnp.take_along_axis(before, route_ids, axis=2).astype(jnp.int32)
    grid_shape = (BATCH, TOK_DEV, TOPK)
    seq_index = jnp.broadcast_to(jnp.arange(BATCH, dtype=jnp.int32)[:, None, None], grid_shape)
    tok_index = jnp.broadcast_to(jnp.arange(TOK_DEV, dtype=jnp.int32)[None, :, None], grid_shape)
    route_index = jnp.broadcast_to(jnp.arange(TOPK, dtype=jnp.int32)[None, None, :], grid_shape)
    slot_tok = jnp.full((BATCH, EXPERTS, CAP), TOK_DEV, jnp.int32).at[seq_index, route_ids, slot_rank].set(tok_index)
    slot_gate = jnp.zeros((BATCH, EXPERTS, CAP), jnp.float32).at[seq_index, route_ids, slot_rank].set(gate_rows)
    slot_route = jnp.zeros((BATCH, EXPERTS, CAP), jnp.int32).at[seq_index, route_ids, slot_rank].set(route_index)
    padded = jnp.concatenate([tokens.reshape(BATCH, TOK_DEV, D), jnp.zeros((BATCH, 1, D), tokens.dtype)], axis=1)
    seq_column = jnp.arange(BATCH, dtype=jnp.int32)[:, None]
    expert_range = jnp.arange(EXPERTS, dtype=jnp.int32)

    def expert_inputs(expert_pos):
        slot_rows = slot_tok[:, expert_pos]
        rows_in = padded[seq_column, slot_rows].reshape(BATCH * CAP, D)
        return (slot_rows, rows_in, w_gate[expert_pos], w_up[expert_pos], w_down[expert_pos])

    def forward_step(mixed_sum, expert_pos):
        slot_rows, rows_in, gate_one, up_one, down_one = expert_inputs(expert_pos)
        expert_out = expert_forward(rows_in, gate_one, up_one, down_one)[4]
        scaled = slot_gate[:, expert_pos][:, :, None] * expert_out.astype(jnp.float32).reshape(BATCH, CAP, D)
        return (mixed_sum.at[seq_column, slot_rows].add(scaled), None)
    mixed_sum, ignored = lax.scan(forward_step, jnp.zeros((BATCH, TOK_DEV + 1, D), jnp.float32), expert_range)
    mixed_rows = tokens.reshape(BATCH, TOK_DEV, D).astype(jnp.float32) + mixed_sum[:, :TOK_DEV]
    pooled = lax.optimization_barrier(jnp.mean(mixed_rows, axis=1))
    inv_rms = lax.rsqrt(lax.optimization_barrier(jnp.mean(pooled * pooled, axis=1)) + 1e-06)
    embedding = (pooled * inv_rms[:, None]).astype(jnp.bfloat16)
    all_embed = embedding.astype(jnp.float32)
    scores = score_scale / D * jnp.dot(all_embed, all_embed.T, precision=highest)
    batch_iota = jnp.arange(BATCH, dtype=jnp.int32)
    others = batch_iota[:, None] != batch_iota[None, :]
    log_total = jnp.log(lax.optimization_barrier(jnp.sum(jnp.where(others, jnp.exp(scores), 0.0), axis=1)))
    partner_score = jnp.take_along_axis(scores, partner[:, None].astype(jnp.int32), axis=1)[:, 0]
    contrast_loss = jnp.mean(log_total - partner_score)
    partner_hit = (batch_iota[None, :] == partner[:, None]).astype(jnp.float32)
    weight = jnp.where(others, jnp.exp(scores - log_total[:, None]), 0.0) - partner_hit
    embed_grad = score_scale / D * (jnp.dot(weight, all_embed, precision=highest) + jnp.dot(weight.T, all_embed, precision=highest))
    seq_grad = inv_rms[:, None] * embed_grad - (inv_rms ** 3 * lax.optimization_barrier(jnp.sum(pooled * embed_grad, axis=1)) / D)[:, None] * pooled

    def backward_step(carry, expert_pos):
        grad_sum, gate_sum = carry
        slot_rows, rows_in, gate_one, up_one, down_one = expert_inputs(expert_pos)
        pre_gate, pre_up, activated, derivative, expert_out = expert_forward(rows_in, gate_one, up_one, down_one)
        out_rows = expert_out.astype(jnp.float32).reshape(BATCH, CAP, D)
        gate_part = lax.optimization_barrier(jnp.sum(out_rows * seq_grad[:, None, :], axis=2))
        gate_sum = gate_sum.at[seq_column, slot_rows, slot_route[:, expert_pos]].add(gate_part)
        out_grad = (slot_gate[:, expert_pos][:, :, None] * seq_grad[:, None, :]).astype(jnp.bfloat16).reshape(BATCH * CAP, D)
        hidden_grad = jnp.dot(out_grad, down_one.T, preferred_element_type=jnp.float32)
        gate_side = (hidden_grad * pre_up * derivative).astype(jnp.bfloat16)
        up_side = (hidden_grad * activated).astype(jnp.bfloat16)
        route_grad = (jnp.dot(gate_side, gate_one.T, preferred_element_type=jnp.float32) + jnp.dot(up_side, up_one.T, preferred_element_type=jnp.float32)).astype(jnp.bfloat16)
        grad_sum = grad_sum.at[seq_column, slot_rows].add(route_grad.astype(jnp.float32).reshape(BATCH, CAP, D))
        return ((grad_sum, gate_sum), None)
    start = (jnp.zeros((BATCH, TOK_DEV + 1, D), jnp.float32), jnp.zeros((BATCH, TOK_DEV + 1, TOPK), jnp.float32))
    (grad_sum, gate_sum), ignored = lax.scan(backward_step, start, expert_range)
    token_grad = (seq_grad[:, None, :] + grad_sum[:, :TOK_DEV]).astype(jnp.bfloat16).reshape(TOKENS, D)
    gate_grad = gate_sum[:, :TOK_DEV].reshape(TOKENS, TOPK)
    return (contrast_loss, token_grad, gate_grad)
```

```python
import jax
import jax.numpy as jnp
from jax import lax
from jax.experimental import pallas as pl
from jax.experimental.pallas import tpu as pltpu
from jax.sharding import PartitionSpec as P

score_scale = 20.0
highest = lax.Precision.HIGHEST


def silu_parts(pre_act):
    sigmoid_val = jax.nn.sigmoid(pre_act)
    return (pre_act * sigmoid_val, sigmoid_val * (1.0 + pre_act * (1.0 - sigmoid_val)))


def expert_forward(slot_piece, gate_full, up_full, down_full):
    pre_gate = jnp.einsum(
        "encd,edf->encf", slot_piece, gate_full, preferred_element_type=jnp.float32
    )
    pre_up = jnp.einsum("encd,edf->encf", slot_piece, up_full, preferred_element_type=jnp.float32)
    activated, derivative = silu_parts(pre_gate)
    hidden = (activated * pre_up).astype(jnp.bfloat16)
    expert_out = jnp.einsum(
        "encf,efd->encd", hidden, down_full, preferred_element_type=jnp.float32
    ).astype(jnp.bfloat16)
    return (expert_out, pre_gate, pre_up)


def on_device(tokens, expert_ids, gate_values, w_gate, w_up, w_down, partner):
    tok_rows, model_width = tokens.shape
    route_count = expert_ids.shape[1]
    local_experts = w_gate.shape[0]
    experts = lax.axis_size("expert") * local_experts
    capacity = tok_rows * route_count // experts + max(1, tok_rows * route_count // (16 * experts))
    slot_total = experts * capacity
    gate_full, up_full, down_full = (
        lax.all_gather(w_gate, "dp", axis=1, tiled=True),
        lax.all_gather(w_up, "dp", axis=1, tiled=True),
        lax.all_gather(w_down, "dp", axis=1, tiled=True),
    )
    expert_iota = jnp.arange(experts, dtype=jnp.int32)
    matches = expert_ids[:, :, None] == expert_iota
    chosen = jnp.sum(matches.astype(jnp.int32), axis=1, dtype=jnp.int32)
    chosen_gate = jnp.sum(jnp.where(matches, gate_values[:, :, None], 0.0), axis=1)
    before = jnp.cumsum(chosen, axis=0, dtype=jnp.int32) - chosen
    slot_rank = jnp.take_along_axis(before, expert_ids, axis=1)
    slot_row = (expert_ids * capacity + slot_rank).reshape(-1)
    slot_iota = jnp.arange(capacity, dtype=jnp.int32)
    onehot = (chosen.T[:, None, :] == 1) & (before.T[:, None, :] == slot_iota[None, :, None])
    placer = onehot.astype(jnp.bfloat16)
    slot_gate = jnp.sum(jnp.where(onehot, chosen_gate.T[:, None, :], 0.0), axis=2)
    outgoing = jnp.einsum("ect,td->ecd", placer, tokens, preferred_element_type=jnp.float32).astype(
        jnp.bfloat16
    )
    outgoing = outgoing.reshape(experts, 1, capacity, model_width)
    placer_flat = placer.reshape(slot_total, tok_rows)
    out_here, pre_gate, pre_up = expert_forward(
        lax.all_to_all(outgoing, "expert", split_axis=0, concat_axis=1, tiled=True),
        gate_full,
        up_full,
        down_full,
    )
    returned_out = lax.all_to_all(
        out_here, "expert", split_axis=1, concat_axis=0, tiled=True
    ).reshape(slot_total, model_width)
    weighted_sum = jnp.dot(
        slot_gate.reshape(slot_total), returned_out.astype(jnp.float32), precision=highest
    )
    pooled = jnp.mean(tokens.astype(jnp.float32), axis=0) + weighted_sum / tok_rows
    inv_rms = lax.rsqrt(jnp.mean(pooled * pooled) + 1e-06)
    embedding = (pooled * inv_rms).astype(jnp.bfloat16)[None, :]
    gathered = lax.all_gather(embedding, ("dp", "expert"), axis=0, tiled=True)
    batch_size = gathered.shape[0]
    own_index = lax.axis_index(("dp", "expert"))
    batch_iota = jnp.arange(batch_size, dtype=jnp.int32)
    scores = (
        score_scale
        / model_width
        * jnp.dot(gathered, embedding[0], preferred_element_type=jnp.float32)
    )
    others = batch_iota != own_index
    log_total = jnp.log(jnp.sum(jnp.where(others, jnp.exp(scores), 0.0)))
    own_partner = lax.dynamic_index_in_dim(partner, own_index, keepdims=False)
    partner_hit = (batch_iota == own_partner).astype(jnp.float32)
    weight = jnp.where(others, jnp.exp(scores - log_total), 0.0) - partner_hit
    all_embed = gathered.astype(jnp.float32)
    row_term = jnp.dot(weight, all_embed, precision=highest)
    all_totals = lax.all_gather(log_total[None], ("dp", "expert"), axis=0, tiled=True)
    column_weight = jnp.where(others, jnp.exp(scores - all_totals), 0.0) - (
        partner == own_index
    ).astype(jnp.float32)
    embed_grad = (
        score_scale
        / model_width
        * (row_term + jnp.dot(column_weight, all_embed, precision=highest))
    )
    partner_rows = jnp.take(gathered, partner, axis=0)
    partner_score = (
        score_scale
        / model_width
        * jnp.einsum("bd,bd->b", gathered, partner_rows, preferred_element_type=jnp.float32)
    )
    contrast_loss = jnp.mean(all_totals - partner_score)
    seq_grad = (
        inv_rms * embed_grad - inv_rms**3 * jnp.sum(pooled * embed_grad) / model_width * pooled
    )
    slot_dots = jnp.dot(returned_out.astype(jnp.float32), seq_grad, precision=highest)
    gate_grad = jnp.take(slot_dots, slot_row, axis=0).reshape(tok_rows, route_count)
    out_grad = (
        (slot_gate[:, :, None] * seq_grad)
        .astype(jnp.bfloat16)
        .reshape(experts, 1, capacity, model_width)
    )
    arrived = lax.all_to_all(out_grad, "expert", split_axis=0, concat_axis=1, tiled=True)
    hidden_grad = jnp.einsum(
        "encd,efd->encf", arrived, down_full, preferred_element_type=jnp.float32
    )
    activated, derivative = silu_parts(pre_gate)
    gate_side = (hidden_grad * pre_up * derivative).astype(jnp.bfloat16)
    up_side = (hidden_grad * activated).astype(jnp.bfloat16)
    route_here = jnp.einsum(
        "encf,edf->encd", gate_side, gate_full, preferred_element_type=jnp.float32
    )
    route_here = (
        route_here
        + jnp.einsum("encf,edf->encd", up_side, up_full, preferred_element_type=jnp.float32)
    ).astype(jnp.bfloat16)
    returned = lax.all_to_all(
        route_here, "expert", split_axis=1, concat_axis=0, tiled=True
    ).reshape(slot_total, model_width)
    route_sum = jnp.einsum("st,sd->td", placer_flat, returned, preferred_element_type=jnp.float32)
    token_grad = (seq_grad + route_sum).astype(jnp.bfloat16)
    return (contrast_loss, token_grad, gate_grad)


mesh_ids = pl.DeviceIdType.MESH
f32 = jnp.float32
bf16 = jnp.bfloat16


def split_dot(lhs, rhs, dims):
    rows = lhs.shape[0]
    high = lhs.astype(bf16)
    low = (lhs - high.astype(f32)).astype(bf16)
    both = lax.dot_general(
        jnp.concatenate([high, low], axis=0), rhs, (dims, ((), ())), preferred_element_type=f32
    )
    return both[:rows] + both[rows:]


def fused_kernel(
    tok_ref, ids_ref, gv_ref, wg_ref, wu_ref, wd_ref, prow_ref, pcol_ref,
    loss_ref, tg_ref, gg_ref,
    tokb, gateb, wbuf, wpad, acc, hid, side, hbar, part, rsb, arb, pool, sgrad, vsend, vrecv, vown,
    ggsend, ggrecv, rb, sibb, sumb, inb,
    tok_s, tok_r, gate_s, gate_r, up_s, dn_s, w_r, hb_s, hb_r, rs_s, rs_r, ar_s, ar_r, ag_s, ag_r,
    v_s, v_r, gg_s, gg_r, sib_s, sib_r, ret_s, ret_r,
):
    p = lax.axis_index("dp")
    q = lax.axis_index("expert")
    n_dp = wbuf.shape[0]
    n_ex = gateb.shape[0]
    rows, width = tok_ref.shape
    ff = wg_ref.shape[2]
    chips = n_ex // 2
    chip = q // 2
    core = q % 2
    batch = n_dp * n_ex
    own = p * n_ex + q
    quarter = wbuf.shape[1]
    ff_part = wd_ref.shape[1]
    cols = width // n_ex
    topk = ids_ref.shape[1]
    experts = gateb.shape[2]

    def ex_peer(i):
        return (q + i) % n_ex

    def ex_from(i):
        return (q + n_ex - i) % n_ex

    def dp_peer(i):
        return (p + i) % n_dp

    def dp_from(i):
        return (p + n_dp - i) % n_dp

    def send(src, dst, s_sem, r_sem, **where):
        return pltpu.make_async_remote_copy(
            src_ref=src, dst_ref=dst, send_sem=s_sem, recv_sem=r_sem,
            device_id=(where.get("dp", p), where.get("ex", q)), device_id_type=mesh_ids,
        )

    barrier = pltpu.get_barrier_semaphore()
    for i in range(1, n_ex):
        pl.semaphore_signal(barrier, inc=1, device_id=(p, ex_peer(i)), device_id_type=mesh_ids)
    for i in range(1, n_dp):
        pl.semaphore_signal(barrier, inc=1, device_id=(dp_peer(i), q), device_id_type=mesh_ids)
    for e in range(2):
        wbuf[p, :, 2 * e * ff : (2 * e + 1) * ff] = wg_ref[e]
        wbuf[p, :, (2 * e + 1) * ff : (2 * e + 2) * ff] = wu_ref[e]
    pl.semaphore_wait(barrier, n_ex + n_dp - 2)

    def up_copy(j):
        return send(wbuf.at[j], wbuf.at[j], up_s.at[j], w_r.at[j], dp=jnp.minimum(p + 1, n_dp - 1))

    def dn_copy(j):
        return send(wbuf.at[j], wbuf.at[j], dn_s.at[j], w_r.at[j], dp=jnp.maximum(p - 1, 0))

    @pl.when(p < n_dp - 1)
    def _():
        up_copy(p).start()

    @pl.when(p > 0)
    def _():
        dn_copy(p).start()

    own_rows = pl.ds(pl.multiple_of(q * rows, rows), rows)
    tok_copies = []
    for i in range(1, n_ex):
        copy = send(tok_ref, tokb.at[own_rows, :], tok_s.at[i], tok_r.at[i], ex=ex_peer(i))
        copy.start()
        tok_copies.append(copy)
    tokb[own_rows, :] = tok_ref[...]

    expert_lane = lax.broadcasted_iota(jnp.int32, (rows, experts), 1)
    gates = jnp.zeros((rows, experts), f32)
    for k in range(topk):
        gates = gates + jnp.where(ids_ref[:, k : k + 1] == expert_lane, gv_ref[:, k : k + 1], 0.0)
    gateb[q] = gates
    gate_copies = []
    for i in range(1, n_ex):
        copy = send(gateb.at[q], gateb.at[q], gate_s.at[i], gate_r.at[i], ex=ex_peer(i))
        copy.start()
        gate_copies.append(copy)

    wpad[...] = jnp.zeros_like(wpad)
    for e in range(2):
        wpad[pl.ds(pl.multiple_of(e * ff + p * ff_part, 32), ff_part), :] = wd_ref[e]
    ggsend[...] = jnp.zeros_like(ggsend)

    for i in range(1, n_ex):
        tok_copies[i - 1].wait_recv()
        gate_copies[i - 1].wait_recv()

    def multiply(j, first):
        d_cols = pl.ds(pl.multiple_of(j * quarter, quarter), quarter)

        def body(n, carry):
            f_cols = pl.ds(pl.multiple_of(n * 256, 256), 256)
            product = jnp.dot(tokb[:, d_cols], wbuf[j, :, f_cols], preferred_element_type=f32)
            if first:
                acc[:, f_cols] = product
            else:
                acc[:, f_cols] += product
            return carry

        lax.fori_loop(0, 4 * ff // 256, body, 0)

    multiply(p, True)
    for k in range(1, n_dp):
        low, high = p - k, p + k

        @pl.when(low >= 0)
        def _():
            up_copy(low).wait_recv()

            @pl.when(p < n_dp - 1)
            def _():
                up_copy(low).start()

        @pl.when(high < n_dp)
        def _():
            dn_copy(high).wait_recv()

            @pl.when(p > 0)
            def _():
                dn_copy(high).start()

        @pl.when(low >= 0)
        def _():
            multiply(low, False)

        @pl.when(high < n_dp)
        def _():
            multiply(high, False)

    def gate_column(s, e):
        return jnp.sum(jnp.where(expert_lane == 2 * q + e, gateb[s], 0.0), axis=1, keepdims=True)

    def forward(s, carry):
        rs = pl.ds(pl.multiple_of(s * rows, rows), rows)
        for e in range(2):
            pre_gate = acc[rs, 2 * e * ff : (2 * e + 1) * ff]
            pre_up = acc[rs, (2 * e + 1) * ff : (2 * e + 2) * ff]
            hidden = (pre_gate * jax.nn.sigmoid(pre_gate) * pre_up).astype(bf16)
            hid[rs, e * ff : (e + 1) * ff] = hidden
            hbar[p, pl.ds(s, 1), e * ff : (e + 1) * ff] = jnp.sum(
                gate_column(s, e) * hidden.astype(f32), axis=0, keepdims=True
            )
        return carry

    lax.fori_loop(0, n_ex, forward, 0)
    hb_copies = []
    for i in range(1, n_dp):
        copy = send(hbar.at[p], hbar.at[p], hb_s.at[i], hb_r.at[i], dp=dp_peer(i))
        copy.start()
        hb_copies.append(copy)

    def factors(s, carry):
        rs = pl.ds(pl.multiple_of(s * rows, rows), rows)
        for e in range(2):
            pre_gate = acc[rs, 2 * e * ff : (2 * e + 1) * ff]
            pre_up = acc[rs, (2 * e + 1) * ff : (2 * e + 2) * ff]
            activated, derivative = silu_parts(pre_gate)
            gate = gate_column(s, e)
            acc[rs, 2 * e * ff : (2 * e + 1) * ff] = gate * pre_up * derivative
            acc[rs, (2 * e + 1) * ff : (2 * e + 2) * ff] = gate * activated
        return carry

    token_mean = jnp.sum(tok_ref[...].astype(f32), axis=0, keepdims=True) / rows
    for copy in hb_copies:
        copy.wait_recv()
    own_row = lax.broadcasted_iota(jnp.int32, (batch, 1), 0) == own
    part[...] = split_dot(
        hbar[...].reshape(batch, 2 * ff), wpad[...], ((1,), (0,))
    ) / rows + jnp.where(own_row, token_mean, 0.0)

    def col_at(i):
        return pl.ds(pl.multiple_of(i * cols, cols), cols)

    rs_copies = []
    for i in range(1, n_ex):
        copy = send(part.at[:, col_at(ex_peer(i))], rsb.at[i], rs_s.at[i], rs_r.at[i], ex=ex_peer(i))
        copy.start()
        rs_copies.append(copy)
    lax.fori_loop(0, n_ex // 2, factors, 0)
    total = part[:, col_at(q)]
    for i in range(1, n_ex):
        rs_copies[i - 1].wait_recv()
        total = total + rsb[i]
    arb[p] = total
    ar_copies = []
    for i in range(1, n_dp):
        copy = send(arb.at[p], arb.at[p], ar_s.at[i], ar_r.at[i], dp=dp_peer(i))
        copy.start()
        ar_copies.append(copy)
    lax.fori_loop(n_ex // 2, n_ex, factors, 0)
    for copy in ar_copies:
        copy.wait_recv()
    total = arb[0]
    for j in range(1, n_dp):
        total = total + arb[j]
    pool[:, col_at(q)] = total
    ag_copies = []
    for i in range(1, n_ex):
        copy = send(pool.at[:, col_at(q)], pool.at[:, col_at(q)], ag_s.at[i], ag_r.at[i], ex=ex_peer(i))
        copy.start()
        ag_copies.append(copy)
    for copy in ag_copies:
        copy.wait_recv()

    pooled = pool[...]
    inv_rms = lax.rsqrt(jnp.sum(pooled * pooled, axis=1, keepdims=True) / width + 1e-06)
    embedding = (pooled * inv_rms).astype(bf16)
    scale = score_scale / width
    scores = scale * lax.dot_general(
        embedding, embedding, (((1,), (1,)), ((), ())), preferred_element_type=f32
    )
    row_id = lax.broadcasted_iota(jnp.int32, (batch, batch), 0)
    col_id = lax.broadcasted_iota(jnp.int32, (batch, batch), 1)
    others = row_id != col_id
    exps = jnp.where(others, jnp.exp(scores), 0.0)
    log_total = jnp.log(jnp.sum(exps, axis=1, keepdims=True))
    log_total_row = jnp.log(jnp.sum(exps, axis=0, keepdims=True))
    hit = (pcol_ref[...] == col_id).astype(f32)
    hit_turned = (prow_ref[...] == row_id).astype(f32)
    partner_score = jnp.sum(scores * hit, axis=1, keepdims=True)
    loss_ref[...] = jnp.sum(log_total - partner_score, axis=0, keepdims=True) / batch
    both = (
        jnp.where(others, jnp.exp(scores - log_total) + jnp.exp(scores - log_total_row), 0.0)
        - hit
        - hit_turned
    )
    embed_grad = scale * split_dot(both, embedding, ((1,), (0,)))
    seq_grad = (
        inv_rms * embed_grad
        - inv_rms * inv_rms * inv_rms
        * (jnp.sum(pooled * embed_grad, axis=1, keepdims=True) / width)
        * pooled
    )
    sgrad[...] = seq_grad
    vpart = split_dot(seq_grad, wpad[...], ((1,), (1,)))
    for j in range(n_dp):
        vsend[j] = vpart[j * n_ex : (j + 1) * n_ex]
    v_copies = []
    for i in range(1, n_dp):
        copy = send(vsend.at[dp_peer(i)], vrecv.at[i], v_s.at[i], v_r.at[i], dp=dp_peer(i))
        copy.start()
        v_copies.append(copy)
    total = vsend[p]
    for i in range(1, n_dp):
        v_copies[i - 1].wait_recv()
        total = total + vrecv[i]
    vown[...] = total

    def sides(s):
        rs = pl.ds(pl.multiple_of(s * rows, rows), rows)
        for e in range(2):
            v_row = vown[pl.ds(s, 1), e * ff : (e + 1) * ff]
            for m in range(2):
                c = slice((2 * e + m) * ff, (2 * e + m + 1) * ff)
                side[rs, c] = (acc[rs, c] * v_row).astype(bf16)

    sibling = chip * 2 + 1 - core
    keep = pl.ds(pl.multiple_of(core * rows, rows), rows)
    give = pl.ds(pl.multiple_of((1 - core) * rows, rows), rows)
    order = list(range(1, chips)) + [0]

    def sib_copy(i):
        return send(rb.at[i, give, :], sibb.at[i], sib_s.at[i], sib_r.at[i], ex=sibling)

    def ret_copy(i):
        return send(sumb.at[i], inb.at[i], ret_s.at[i], ret_r.at[i], ex=((chip + i) % chips) * 2 + core)

    def finish(i):
        sib_copy(i).wait_recv()
        summed = rb[i, keep, :].astype(f32) + sibb[i].astype(f32)
        if i:
            sumb[i] = summed.astype(bf16)
            ret_copy(i).start()
            return None
        return summed

    for step, i in enumerate(order):
        target = (chip + i) % chips
        sides(2 * target)
        sides(2 * target + 1)
        pair = pl.ds(pl.multiple_of(target * 2 * rows, 2 * rows), 2 * rows)

        def back(j, carry, i=i, pair=pair):
            rb[i, :, pl.ds(pl.multiple_of(j * quarter, quarter), quarter)] = lax.dot_general(
                side[pair, :], wbuf[j], (((1,), (1,)), ((), ())), preferred_element_type=f32
            ).astype(bf16)
            return carry

        lax.fori_loop(0, n_dp, back, 0)
        sib_copy(i).start()
        if step:
            finish(order[step - 1])

    lane = lax.broadcasted_iota(jnp.int32, (n_ex, n_ex * rows), 1)
    block_diag = lane // rows == lax.broadcasted_iota(jnp.int32, (n_ex, n_ex * rows), 0)
    for e in range(2):
        dots = split_dot(
            vown[:, e * ff : (e + 1) * ff], hid[:, e * ff : (e + 1) * ff], ((1,), (1,))
        )
        ggsend[e : e + 1, :] = jnp.sum(jnp.where(block_diag, dots, 0.0), axis=0, keepdims=True)

    def seq_cols(i):
        return pl.ds(pl.multiple_of(i * rows, rows), rows)

    gg_copies = []
    for i in range(1, n_ex):
        copy = send(ggsend.at[:, seq_cols(ex_peer(i))], ggrecv.at[q], gg_s.at[i], gg_r.at[i], ex=ex_peer(i))
        copy.start()
        gg_copies.append(copy)
    ggrecv[q] = ggsend[:, seq_cols(q)]
    grad = finish(0) + sgrad[pl.ds(own, 1), :]
    for copy in gg_copies:
        copy.wait_recv()
    all_dots = ggrecv[...].reshape(n_ex * 8, rows).T
    dot_lane = lax.broadcasted_iota(jnp.int32, (rows, n_ex * 8), 1)
    lane_expert = jnp.where(dot_lane % 8 < 2, dot_lane // 8 * 2 + dot_lane % 8, -1)
    route_lane = lax.broadcasted_iota(jnp.int32, (rows, topk), 1)
    result = jnp.zeros((rows, topk), f32)
    for k in range(topk):
        picked = jnp.sum(
            jnp.where(ids_ref[:, k : k + 1] == lane_expert, all_dots, 0.0), axis=1, keepdims=True
        )
        result = jnp.where(route_lane == k, picked, result)
    gg_ref[...] = result
    for i in range(1, chips):
        ret_copy(i).wait_recv()
        grad = grad + inb[i].astype(f32)
    tg_ref[...] = grad.astype(bf16)

    for copies in (tok_copies, gate_copies, hb_copies, rs_copies, ar_copies, ag_copies, v_copies, gg_copies):
        for copy in copies:
            copy.wait_send()
    for i in range(chips):
        sib_copy(i).wait_send()
        if i:
            ret_copy(i).wait_send()
    for k in range(n_dp):
        low, high = p - k, p + k

        @pl.when((low >= 0) & (p < n_dp - 1))
        def _():
            up_copy(low).wait_send()

        @pl.when((high < n_dp) & (p > 0))
        def _():
            dn_copy(high).wait_send()


def fused(tokens, expert_ids, gate_values, w_gate, w_up, w_down, partner):
    rows, width = tokens.shape
    topk = expert_ids.shape[1]
    ff = w_gate.shape[2]
    n_dp, n_ex = lax.axis_size("dp"), lax.axis_size("expert")
    batch = n_dp * n_ex
    all_rows = n_ex * rows
    cols = width // n_ex
    chips = n_ex // 2
    dma = pltpu.SemaphoreType.DMA
    vmem = pl.BlockSpec(memory_space=pltpu.VMEM)
    loss, token_grad, gate_grad = pl.pallas_call(
        fused_kernel,
        out_shape=(
            jax.ShapeDtypeStruct((1, 1), f32),
            jax.ShapeDtypeStruct((rows, width), bf16),
            jax.ShapeDtypeStruct((rows, topk), f32),
        ),
        in_specs=[vmem] * 8,
        out_specs=(vmem, vmem, vmem),
        scratch_shapes=[
            pltpu.VMEM((all_rows, width), bf16),
            pltpu.VMEM((n_ex, rows, 2 * n_ex), f32),
            pltpu.VMEM((n_dp, width // n_dp, 4 * ff), bf16),
            pltpu.VMEM((2 * ff, width), bf16),
            pltpu.VMEM((all_rows, 4 * ff), f32),
            pltpu.VMEM((all_rows, 2 * ff), bf16),
            pltpu.VMEM((all_rows, 4 * ff), bf16),
            pltpu.VMEM((n_dp, n_ex, 2 * ff), f32),
            pltpu.VMEM((batch, width), f32),
            pltpu.VMEM((n_ex, batch, cols), f32),
            pltpu.VMEM((n_dp, batch, cols), f32),
            pltpu.VMEM((batch, width), f32),
            pltpu.VMEM((batch, width), f32),
            pltpu.VMEM((n_dp, n_ex, 2 * ff), f32),
            pltpu.VMEM((n_dp, n_ex, 2 * ff), f32),
            pltpu.VMEM((n_ex, 2 * ff), f32),
            pltpu.VMEM((8, all_rows), f32),
            pltpu.VMEM((n_ex, 8, rows), f32),
            pltpu.VMEM((chips, 2 * rows, width), bf16),
            pltpu.VMEM((chips, rows, width), bf16),
            pltpu.VMEM((chips, rows, width), bf16),
            pltpu.VMEM((chips, rows, width), bf16),
        ]
        + [dma((n_ex,))] * 4
        + [dma((n_dp,))] * 3
        + [dma((n_dp,))] * 2
        + [dma((n_ex,))] * 2
        + [dma((n_dp,))] * 2
        + [dma((n_ex,))] * 2
        + [dma((n_dp,))] * 2
        + [dma((n_ex,))] * 2
        + [dma((chips,))] * 4,
        compiler_params=pltpu.CompilerParams(
            collective_id=0, has_side_effects=True, vmem_limit_bytes=48 * 1024 * 1024
        ),
    )(tokens, expert_ids, gate_values, w_gate, w_up, w_down, partner[None, :], partner[:, None])
    return (loss[0, 0], token_grad, gate_grad)


def fits_fused(mesh):
    return mesh.shape["dp"] == 4 and mesh.shape["expert"] == 8


def solution(mesh):
    placed = (
        P(("dp", "expert"), None),
        P(("dp", "expert"), None),
        P(("dp", "expert"), None),
        P("expert", "dp", None),
        P("expert", "dp", None),
        P("expert", "dp", None),
        P(),
    )
    return jax.shard_map(
        fused if fits_fused(mesh) else on_device,
        mesh=mesh,
        in_specs=placed,
        out_specs=(P(), P(("dp", "expert"), None), P(("dp", "expert"), None)),
        check_vma=False,
    )
```

```python
import jax
import jax.numpy as jnp
from jax import lax
from jax.experimental import pallas as pl
from jax.experimental.pallas import tpu as pltpu
from jax.sharding import PartitionSpec as P

score_scale = 20.0
highest = lax.Precision.HIGHEST


def silu_parts(pre_act):
    sigmoid_val = jax.nn.sigmoid(pre_act)
    return (pre_act * sigmoid_val, sigmoid_val * (1.0 + pre_act * (1.0 - sigmoid_val)))


def expert_forward(slot_piece, gate_full, up_full, down_full):
    pre_gate = jnp.einsum(
        "encd,edf->encf", slot_piece, gate_full, preferred_element_type=jnp.float32
    )
    pre_up = jnp.einsum("encd,edf->encf", slot_piece, up_full, preferred_element_type=jnp.float32)
    activated, derivative = silu_parts(pre_gate)
    hidden = (activated * pre_up).astype(jnp.bfloat16)
    expert_out = jnp.einsum(
        "encf,efd->encd", hidden, down_full, preferred_element_type=jnp.float32
    ).astype(jnp.bfloat16)
    return (expert_out, pre_gate, pre_up)


def on_device(tokens, expert_ids, gate_values, w_gate, w_up, w_down, partner):
    tok_rows, model_width = tokens.shape
    route_count = expert_ids.shape[1]
    local_experts = w_gate.shape[0]
    experts = lax.axis_size("expert") * local_experts
    capacity = tok_rows * route_count // experts + max(1, tok_rows * route_count // (16 * experts))
    slot_total = experts * capacity
    gate_full, up_full, down_full = (
        lax.all_gather(w_gate, "dp", axis=1, tiled=True),
        lax.all_gather(w_up, "dp", axis=1, tiled=True),
        lax.all_gather(w_down, "dp", axis=1, tiled=True),
    )
    expert_iota = jnp.arange(experts, dtype=jnp.int32)
    matches = expert_ids[:, :, None] == expert_iota
    chosen = jnp.sum(matches.astype(jnp.int32), axis=1, dtype=jnp.int32)
    chosen_gate = jnp.sum(jnp.where(matches, gate_values[:, :, None], 0.0), axis=1)
    before = jnp.cumsum(chosen, axis=0, dtype=jnp.int32) - chosen
    slot_rank = jnp.take_along_axis(before, expert_ids, axis=1)
    slot_row = (expert_ids * capacity + slot_rank).reshape(-1)
    slot_iota = jnp.arange(capacity, dtype=jnp.int32)
    onehot = (chosen.T[:, None, :] == 1) & (before.T[:, None, :] == slot_iota[None, :, None])
    placer = onehot.astype(jnp.bfloat16)
    slot_gate = jnp.sum(jnp.where(onehot, chosen_gate.T[:, None, :], 0.0), axis=2)
    outgoing = jnp.einsum("ect,td->ecd", placer, tokens, preferred_element_type=jnp.float32).astype(
        jnp.bfloat16
    )
    outgoing = outgoing.reshape(experts, 1, capacity, model_width)
    placer_flat = placer.reshape(slot_total, tok_rows)
    out_here, pre_gate, pre_up = expert_forward(
        lax.all_to_all(outgoing, "expert", split_axis=0, concat_axis=1, tiled=True),
        gate_full,
        up_full,
        down_full,
    )
    returned_out = lax.all_to_all(
        out_here, "expert", split_axis=1, concat_axis=0, tiled=True
    ).reshape(slot_total, model_width)
    weighted_sum = jnp.dot(
        slot_gate.reshape(slot_total), returned_out.astype(jnp.float32), precision=highest
    )
    pooled = jnp.mean(tokens.astype(jnp.float32), axis=0) + weighted_sum / tok_rows
    inv_rms = lax.rsqrt(jnp.mean(pooled * pooled) + 1e-06)
    embedding = (pooled * inv_rms).astype(jnp.bfloat16)[None, :]
    gathered = lax.all_gather(embedding, ("dp", "expert"), axis=0, tiled=True)
    batch_size = gathered.shape[0]
    own_index = lax.axis_index(("dp", "expert"))
    batch_iota = jnp.arange(batch_size, dtype=jnp.int32)
    scores = (
        score_scale
        / model_width
        * jnp.dot(gathered, embedding[0], preferred_element_type=jnp.float32)
    )
    others = batch_iota != own_index
    log_total = jnp.log(jnp.sum(jnp.where(others, jnp.exp(scores), 0.0)))
    own_partner = lax.dynamic_index_in_dim(partner, own_index, keepdims=False)
    partner_hit = (batch_iota == own_partner).astype(jnp.float32)
    weight = jnp.where(others, jnp.exp(scores - log_total), 0.0) - partner_hit
    all_embed = gathered.astype(jnp.float32)
    row_term = jnp.dot(weight, all_embed, precision=highest)
    all_totals = lax.all_gather(log_total[None], ("dp", "expert"), axis=0, tiled=True)
    column_weight = jnp.where(others, jnp.exp(scores - all_totals), 0.0) - (
        partner == own_index
    ).astype(jnp.float32)
    embed_grad = (
        score_scale
        / model_width
        * (row_term + jnp.dot(column_weight, all_embed, precision=highest))
    )
    partner_rows = jnp.take(gathered, partner, axis=0)
    partner_score = (
        score_scale
        / model_width
        * jnp.einsum("bd,bd->b", gathered, partner_rows, preferred_element_type=jnp.float32)
    )
    contrast_loss = jnp.mean(all_totals - partner_score)
    seq_grad = (
        inv_rms * embed_grad - inv_rms**3 * jnp.sum(pooled * embed_grad) / model_width * pooled
    )
    slot_dots = jnp.dot(returned_out.astype(jnp.float32), seq_grad, precision=highest)
    gate_grad = jnp.take(slot_dots, slot_row, axis=0).reshape(tok_rows, route_count)
    out_grad = (
        (slot_gate[:, :, None] * seq_grad)
        .astype(jnp.bfloat16)
        .reshape(experts, 1, capacity, model_width)
    )
    arrived = lax.all_to_all(out_grad, "expert", split_axis=0, concat_axis=1, tiled=True)
    hidden_grad = jnp.einsum(
        "encd,efd->encf", arrived, down_full, preferred_element_type=jnp.float32
    )
    activated, derivative = silu_parts(pre_gate)
    gate_side = (hidden_grad * pre_up * derivative).astype(jnp.bfloat16)
    up_side = (hidden_grad * activated).astype(jnp.bfloat16)
    route_here = jnp.einsum(
        "encf,edf->encd", gate_side, gate_full, preferred_element_type=jnp.float32
    )
    route_here = (
        route_here
        + jnp.einsum("encf,edf->encd", up_side, up_full, preferred_element_type=jnp.float32)
    ).astype(jnp.bfloat16)
    returned = lax.all_to_all(
        route_here, "expert", split_axis=1, concat_axis=0, tiled=True
    ).reshape(slot_total, model_width)
    route_sum = jnp.einsum("st,sd->td", placer_flat, returned, preferred_element_type=jnp.float32)
    token_grad = (seq_grad + route_sum).astype(jnp.bfloat16)
    return (contrast_loss, token_grad, gate_grad)


mesh_ids = pl.DeviceIdType.MESH
f32 = jnp.float32
bf16 = jnp.bfloat16


def split_dot(lhs, rhs, dims):
    rows = lhs.shape[0]
    high = lhs.astype(bf16)
    low = (lhs - high.astype(f32)).astype(bf16)
    both = lax.dot_general(
        jnp.concatenate([high, low], axis=0), rhs, (dims, ((), ())), preferred_element_type=f32
    )
    return both[:rows] + both[rows:]


def fused_kernel(
    tok_ref, ids_ref, gv_ref, wg_ref, wu_ref, wd_ref, prow_ref,
    loss_ref, tg_ref, gg_ref,
    tokb, gateb, gate_t, wbuf, wpad, acc, hid, side, hbar, part, rsb, arb, pool, sgrad, vsend, vrecv, vown,
    ggsend, ggrecv, rb, sibb, sumb, inb,
    loc_s, tok_s, tok_r, gate_s, gate_r, up_s, dn_s, w_r, hb_s, hb_r, rs_s, rs_r, ar_s, ar_r, ag_s, ag_r,
    v_s, v_r, gg_s, gg_r, sib_s, sib_r, ret_s, ret_r,
):
    p = lax.axis_index("dp")
    q = lax.axis_index("expert")
    n_dp = wbuf.shape[0]
    n_ex = gateb.shape[0]
    rows, width = tok_ref.shape
    ff = wg_ref.shape[2]
    chips = n_ex // 2
    chip = q // 2
    core = q % 2
    batch = n_dp * n_ex
    own = p * n_ex + q
    quarter = wbuf.shape[1]
    ff_part = wd_ref.shape[1]
    cols = width // n_ex
    topk = ids_ref.shape[0]
    experts = gateb.shape[1]

    def ex_peer(i):
        return (q + i) % n_ex

    def ex_from(i):
        return (q + n_ex - i) % n_ex

    def dp_peer(i):
        return (p + i) % n_dp

    def dp_from(i):
        return (p + n_dp - i) % n_dp

    def send(src, dst, s_sem, r_sem, **where):
        return pltpu.make_async_remote_copy(
            src_ref=src, dst_ref=dst, send_sem=s_sem, recv_sem=r_sem,
            device_id=(where.get("dp", p), where.get("ex", q)), device_id_type=mesh_ids,
        )

    barrier = pltpu.get_barrier_semaphore()
    for i in range(1, n_ex):
        pl.semaphore_signal(barrier, inc=1, device_id=(p, ex_peer(i)), device_id_type=mesh_ids)
    for i in range(1, n_dp):
        pl.semaphore_signal(barrier, inc=1, device_id=(dp_peer(i), q), device_id_type=mesh_ids)
    weight_loads = []
    for e in range(2):
        for m, ref in enumerate((wg_ref, wu_ref)):
            c = 2 * e + m
            weight_loads.append(
                pltpu.make_async_copy(ref.at[e], wbuf.at[p, :, c * ff : (c + 1) * ff], loc_s.at[c])
            )
    own_rows = pl.ds(pl.multiple_of(q * rows, rows), rows)
    token_load = pltpu.make_async_copy(tok_ref, tokb.at[own_rows, :], loc_s.at[4])
    for load in weight_loads:
        load.start()
    token_load.start()
    wpad[...] = jnp.zeros_like(wpad)
    down_loads = []
    for e in range(2):
        load = pltpu.make_async_copy(
            wd_ref.at[e],
            wpad.at[pl.ds(pl.multiple_of(e * ff + p * ff_part, 32), ff_part), :],
            loc_s.at[5 + e],
        )
        load.start()
        down_loads.append(load)
    for load in weight_loads:
        load.wait()
    pl.semaphore_wait(barrier, n_ex + n_dp - 2)

    half = quarter // 2

    def piece(j, h):
        return wbuf.at[j, h * half : (h + 1) * half, :]

    def up_copy(j, h):
        return send(
            piece(j, h), piece(j, h), up_s.at[j, h], w_r.at[j, h], dp=jnp.minimum(p + 1, n_dp - 1)
        )

    def dn_copy(j, h):
        return send(piece(j, h), piece(j, h), dn_s.at[j, h], w_r.at[j, h], dp=jnp.maximum(p - 1, 0))

    for h in range(2):

        @pl.when(p < n_dp - 1)
        def _(h=h):
            up_copy(p, h).start()

        @pl.when(p > 0)
        def _(h=h):
            dn_copy(p, h).start()

    token_load.wait()
    tok_copies = []
    for i in range(1, n_ex):
        copy = send(tokb.at[own_rows, :], tokb.at[own_rows, :], tok_s.at[i], tok_r.at[i], ex=ex_peer(i))
        copy.start()
        tok_copies.append(copy)

    expert_row = lax.broadcasted_iota(jnp.int32, (experts, rows), 0)
    gates = jnp.zeros((experts, rows), f32)
    for k in range(topk):
        gates = gates + jnp.where(ids_ref[k : k + 1, :] == expert_row, gv_ref[k : k + 1, :], 0.0)
    gateb[q] = gates
    gate_copies = []
    for i in range(1, n_ex):
        copy = send(gateb.at[q], gateb.at[q], gate_s.at[i], gate_r.at[i], ex=ex_peer(i))
        copy.start()
        gate_copies.append(copy)

    ggsend[...] = jnp.zeros_like(ggsend)
    for load in down_loads:
        load.wait()

    def multiply(j, first):
        d_cols = pl.ds(pl.multiple_of(j * quarter, quarter), quarter)

        def body(n, carry):
            f_cols = pl.ds(pl.multiple_of(n * 256, 256), 256)
            product = jnp.dot(tokb[:, d_cols], wbuf[j, :, f_cols], preferred_element_type=f32)
            if first:
                acc[:, f_cols] = product
            else:
                acc[:, f_cols] += product
            return carry

        lax.fori_loop(0, 4 * ff // 256, body, 0)

    def pass_on(k):
        low, high = p - k, p + k
        for h in range(2):

            @pl.when(low >= 0)
            def _(h=h):
                up_copy(low, h).wait_recv()

                @pl.when(p < n_dp - 1)
                def _():
                    up_copy(low, h).start()

            @pl.when(high < n_dp)
            def _(h=h):
                dn_copy(high, h).wait_recv()

                @pl.when(p > 0)
                def _():
                    dn_copy(high, h).start()

    def multiply_step(k):
        low, high = p - k, p + k

        @pl.when(low >= 0)
        def _():
            multiply(low, False)

        @pl.when(high < n_dp)
        def _():
            multiply(high, False)

    pass_on(1)
    for i in range(1, n_ex):
        tok_copies[i - 1].wait_recv()
        gate_copies[i - 1].wait_recv()
    for s in range(n_ex):
        gate_t[s] = gateb[s].T
    multiply(p, True)
    multiply_step(1)
    for k in range(2, n_dp):
        pass_on(k)
        multiply_step(k)

    expert_lane = lax.broadcasted_iota(jnp.int32, (rows, experts), 1)

    def gate_column(s, e):
        return jnp.sum(jnp.where(expert_lane == 2 * q + e, gate_t[s], 0.0), axis=1, keepdims=True)

    def forward(s, carry):
        rs = pl.ds(pl.multiple_of(s * rows, rows), rows)
        for e in range(2):
            pre_gate = acc[rs, 2 * e * ff : (2 * e + 1) * ff]
            pre_up = acc[rs, (2 * e + 1) * ff : (2 * e + 2) * ff]
            hidden = (pre_gate * jax.nn.sigmoid(pre_gate) * pre_up).astype(bf16)
            hid[rs, e * ff : (e + 1) * ff] = hidden
            hbar[p, pl.ds(s, 1), e * ff : (e + 1) * ff] = jnp.sum(
                gate_column(s, e) * hidden.astype(f32), axis=0, keepdims=True
            )
        return carry

    lax.fori_loop(0, n_ex, forward, 0)
    hb_copies = []
    for i in range(1, n_dp):
        copy = send(hbar.at[p], hbar.at[p], hb_s.at[i], hb_r.at[i], dp=dp_peer(i))
        copy.start()
        hb_copies.append(copy)

    def factors(s, carry):
        rs = pl.ds(pl.multiple_of(s * rows, rows), rows)
        for e in range(2):
            pre_gate = acc[rs, 2 * e * ff : (2 * e + 1) * ff]
            pre_up = acc[rs, (2 * e + 1) * ff : (2 * e + 2) * ff]
            activated, derivative = silu_parts(pre_gate)
            gate = gate_column(s, e)
            acc[rs, 2 * e * ff : (2 * e + 1) * ff] = gate * pre_up * derivative
            acc[rs, (2 * e + 1) * ff : (2 * e + 2) * ff] = gate * activated
        return carry

    token_mean = jnp.sum(tokb[own_rows, :].astype(f32), axis=0, keepdims=True) / rows
    for copy in hb_copies:
        copy.wait_recv()
    own_row = lax.broadcasted_iota(jnp.int32, (batch, 1), 0) == own
    part[...] = split_dot(
        hbar[...].reshape(batch, 2 * ff), wpad[...], ((1,), (0,))
    ) / rows + jnp.where(own_row, token_mean, 0.0)

    def col_at(i):
        return pl.ds(pl.multiple_of(i * cols, cols), cols)

    rs_copies = []
    for i in range(1, n_ex):
        copy = send(part.at[:, col_at(ex_peer(i))], rsb.at[i], rs_s.at[i], rs_r.at[i], ex=ex_peer(i))
        copy.start()
        rs_copies.append(copy)
    lax.fori_loop(0, n_ex // 2, factors, 0)
    total = part[:, col_at(q)]
    for i in range(1, n_ex):
        rs_copies[i - 1].wait_recv()
        total = total + rsb[i]
    arb[p] = total
    ar_copies = []
    for i in range(1, n_dp):
        copy = send(arb.at[p], arb.at[p], ar_s.at[i], ar_r.at[i], dp=dp_peer(i))
        copy.start()
        ar_copies.append(copy)
    lax.fori_loop(n_ex // 2, n_ex, factors, 0)
    for copy in ar_copies:
        copy.wait_recv()
    total = arb[0]
    for j in range(1, n_dp):
        total = total + arb[j]
    pool[:, col_at(q)] = total
    ag_copies = []
    for i in range(1, n_ex):
        copy = send(pool.at[:, col_at(q)], pool.at[:, col_at(q)], ag_s.at[i], ag_r.at[i], ex=ex_peer(i))
        copy.start()
        ag_copies.append(copy)
    for copy in ag_copies:
        copy.wait_recv()

    pooled = pool[...]
    inv_rms = lax.rsqrt(jnp.sum(pooled * pooled, axis=1, keepdims=True) / width + 1e-06)
    embedding = (pooled * inv_rms).astype(bf16)
    scale = score_scale / width
    scores = scale * lax.dot_general(
        embedding, embedding, (((1,), (1,)), ((), ())), preferred_element_type=f32
    )
    row_id = lax.broadcasted_iota(jnp.int32, (batch, batch), 0)
    col_id = lax.broadcasted_iota(jnp.int32, (batch, batch), 1)
    others = row_id != col_id
    exps = jnp.where(others, jnp.exp(scores), 0.0)
    log_total = jnp.log(jnp.sum(exps, axis=1, keepdims=True))
    log_total_row = jnp.log(jnp.sum(exps, axis=0, keepdims=True))
    hit_turned = (prow_ref[...] == row_id).astype(f32)
    hit = hit_turned.T
    partner_score = jnp.sum(scores * hit_turned, axis=0, keepdims=True)
    loss_ref[...] = jnp.sum(log_total_row - partner_score, axis=1, keepdims=True) / batch
    both = (
        jnp.where(others, jnp.exp(scores - log_total) + jnp.exp(scores - log_total_row), 0.0)
        - hit
        - hit_turned
    )
    embed_grad = scale * split_dot(both, embedding, ((1,), (0,)))
    seq_grad = (
        inv_rms * embed_grad
        - inv_rms * inv_rms * inv_rms
        * (jnp.sum(pooled * embed_grad, axis=1, keepdims=True) / width)
        * pooled
    )
    sgrad[...] = seq_grad
    vpart = split_dot(seq_grad, wpad[...], ((1,), (1,)))
    for j in range(n_dp):
        vsend[j] = vpart[j * n_ex : (j + 1) * n_ex]
    v_copies = []
    for i in range(1, n_dp):
        copy = send(vsend.at[dp_peer(i)], vrecv.at[i], v_s.at[i], v_r.at[i], dp=dp_peer(i))
        copy.start()
        v_copies.append(copy)
    total = vsend[p]
    for i in range(1, n_dp):
        v_copies[i - 1].wait_recv()
        total = total + vrecv[i]
    vown[...] = total

    def sides(s):
        rs = pl.ds(pl.multiple_of(s * rows, rows), rows)
        for e in range(2):
            v_row = vown[pl.ds(s, 1), e * ff : (e + 1) * ff]
            for m in range(2):
                c = slice((2 * e + m) * ff, (2 * e + m + 1) * ff)
                side[rs, c] = (acc[rs, c] * v_row).astype(bf16)

    sibling = chip * 2 + 1 - core
    keep = pl.ds(pl.multiple_of(core * rows, rows), rows)
    give = pl.ds(pl.multiple_of((1 - core) * rows, rows), rows)
    order = list(range(1, chips)) + [0]

    def sib_copy(i):
        return send(rb.at[i, give, :], sibb.at[i], sib_s.at[i], sib_r.at[i], ex=sibling)

    def ret_copy(i):
        return send(sumb.at[i], inb.at[i], ret_s.at[i], ret_r.at[i], ex=((chip + i) % chips) * 2 + core)

    def finish(i):
        sib_copy(i).wait_recv()
        summed = rb[i, keep, :].astype(f32) + sibb[i].astype(f32)
        if i:
            sumb[i] = summed.astype(bf16)
            ret_copy(i).start()
            return None
        return summed

    for step, i in enumerate(order):
        target = (chip + i) % chips
        sides(2 * target)
        sides(2 * target + 1)
        pair = pl.ds(pl.multiple_of(target * 2 * rows, 2 * rows), 2 * rows)

        def back(j, carry, i=i, pair=pair):
            rb[i, :, pl.ds(pl.multiple_of(j * quarter, quarter), quarter)] = lax.dot_general(
                side[pair, :], wbuf[j], (((1,), (1,)), ((), ())), preferred_element_type=f32
            ).astype(bf16)
            return carry

        lax.fori_loop(0, n_dp, back, 0)
        sib_copy(i).start()
        if step:
            finish(order[step - 1])

    lane = lax.broadcasted_iota(jnp.int32, (n_ex, n_ex * rows), 1)
    block_diag = lane // rows == lax.broadcasted_iota(jnp.int32, (n_ex, n_ex * rows), 0)
    for e in range(2):
        dots = split_dot(
            vown[:, e * ff : (e + 1) * ff], hid[:, e * ff : (e + 1) * ff], ((1,), (1,))
        )
        ggsend[e : e + 1, :] = jnp.sum(jnp.where(block_diag, dots, 0.0), axis=0, keepdims=True)

    def seq_cols(i):
        return pl.ds(pl.multiple_of(i * rows, rows), rows)

    gg_copies = []
    for i in range(1, n_ex):
        copy = send(ggsend.at[:, seq_cols(ex_peer(i))], ggrecv.at[q], gg_s.at[i], gg_r.at[i], ex=ex_peer(i))
        copy.start()
        gg_copies.append(copy)
    ggrecv[q] = ggsend[:, seq_cols(q)]
    grad = finish(0) + sgrad[pl.ds(own, 1), :]
    for copy in gg_copies:
        copy.wait_recv()
    all_dots = ggrecv[...].reshape(n_ex * 8, rows)
    dot_row = lax.broadcasted_iota(jnp.int32, (n_ex * 8, 1), 0)
    row_expert = jnp.where(dot_row % 8 < 2, dot_row // 8 * 2 + dot_row % 8, -1)
    for k in range(topk):
        gg_ref[k : k + 1, :] = jnp.sum(
            jnp.where(ids_ref[k : k + 1, :] == row_expert, all_dots, 0.0), axis=0, keepdims=True
        )
    for i in range(1, chips):
        ret_copy(i).wait_recv()
        grad = grad + inb[i].astype(f32)
    tg_ref[...] = grad.astype(bf16)

    for copies in (tok_copies, gate_copies, hb_copies, rs_copies, ar_copies, ag_copies, v_copies, gg_copies):
        for copy in copies:
            copy.wait_send()
    for i in range(chips):
        sib_copy(i).wait_send()
        if i:
            ret_copy(i).wait_send()
    for k in range(n_dp):
        low, high = p - k, p + k

        for h in range(2):

            @pl.when((low >= 0) & (p < n_dp - 1))
            def _(h=h):
                up_copy(low, h).wait_send()

            @pl.when((high < n_dp) & (p > 0))
            def _(h=h):
                dn_copy(high, h).wait_send()


def fused(tokens, expert_ids, gate_values, w_gate, w_up, w_down, partner):
    rows, width = tokens.shape
    topk = expert_ids.shape[1]
    ff = w_gate.shape[2]
    n_dp, n_ex = lax.axis_size("dp"), lax.axis_size("expert")
    batch = n_dp * n_ex
    all_rows = n_ex * rows
    cols = width // n_ex
    chips = n_ex // 2
    dma = pltpu.SemaphoreType.DMA
    vmem = pl.BlockSpec(memory_space=pltpu.VMEM)
    hbm = pl.BlockSpec(memory_space=pl.ANY)
    loss, token_grad, gate_grad = pl.pallas_call(
        fused_kernel,
        out_shape=(
            jax.ShapeDtypeStruct((1, 1), f32),
            jax.ShapeDtypeStruct((rows, width), bf16),
            jax.ShapeDtypeStruct((topk, rows), f32),
        ),
        in_specs=[hbm, vmem, vmem, hbm, hbm, hbm, vmem],
        out_specs=(vmem, vmem, vmem),
        scratch_shapes=[
            pltpu.VMEM((all_rows, width), bf16),
            pltpu.VMEM((n_ex, 2 * n_ex, rows), f32),
            pltpu.VMEM((n_ex, rows, 2 * n_ex), f32),
            pltpu.VMEM((n_dp, width // n_dp, 4 * ff), bf16),
            pltpu.VMEM((2 * ff, width), bf16),
            pltpu.VMEM((all_rows, 4 * ff), f32),
            pltpu.VMEM((all_rows, 2 * ff), bf16),
            pltpu.VMEM((all_rows, 4 * ff), bf16),
            pltpu.VMEM((n_dp, n_ex, 2 * ff), f32),
            pltpu.VMEM((batch, width), f32),
            pltpu.VMEM((n_ex, batch, cols), f32),
            pltpu.VMEM((n_dp, batch, cols), f32),
            pltpu.VMEM((batch, width), f32),
            pltpu.VMEM((batch, width), f32),
            pltpu.VMEM((n_dp, n_ex, 2 * ff), f32),
            pltpu.VMEM((n_dp, n_ex, 2 * ff), f32),
            pltpu.VMEM((n_ex, 2 * ff), f32),
            pltpu.VMEM((8, all_rows), f32),
            pltpu.VMEM((n_ex, 8, rows), f32),
            pltpu.VMEM((chips, 2 * rows, width), bf16),
            pltpu.VMEM((chips, rows, width), bf16),
            pltpu.VMEM((chips, rows, width), bf16),
            pltpu.VMEM((chips, rows, width), bf16),
        ]
        + [dma((8,))]
        + [dma((n_ex,))] * 4
        + [dma((n_dp, 2))] * 3
        + [dma((n_dp,))] * 2
        + [dma((n_ex,))] * 2
        + [dma((n_dp,))] * 2
        + [dma((n_ex,))] * 2
        + [dma((n_dp,))] * 2
        + [dma((n_ex,))] * 2
        + [dma((chips,))] * 4,
        compiler_params=pltpu.CompilerParams(
            collective_id=0, has_side_effects=True, vmem_limit_bytes=60 * 1024 * 1024
        ),
    )(tokens, expert_ids.T, gate_values.T, w_gate, w_up, w_down, partner[None, :])
    return (loss[0, 0], token_grad, gate_grad.T)


def fits_fused(mesh):
    return mesh.shape["dp"] == 4 and mesh.shape["expert"] == 8


def solution(mesh):
    placed = (
        P(("dp", "expert"), None),
        P(("dp", "expert"), None),
        P(("dp", "expert"), None),
        P("expert", "dp", None),
        P("expert", "dp", None),
        P("expert", "dp", None),
        P(),
    )
    return jax.shard_map(
        fused if fits_fused(mesh) else on_device,
        mesh=mesh,
        in_specs=placed,
        out_specs=(P(), P(("dp", "expert"), None), P(("dp", "expert"), None)),
        check_vma=False,
    )
```

```python
import jax
import jax.numpy as jnp
from jax import lax
from jax.experimental import pallas as pl
from jax.experimental.pallas import tpu as pltpu
from jax.sharding import PartitionSpec as P

score_scale = 20.0
highest = lax.Precision.HIGHEST


def silu_parts(pre_act):
    sigmoid_val = jax.nn.sigmoid(pre_act)
    return (pre_act * sigmoid_val, sigmoid_val * (1.0 + pre_act * (1.0 - sigmoid_val)))


def expert_forward(slot_piece, gate_full, up_full, down_full):
    pre_gate = jnp.einsum(
        "encd,edf->encf", slot_piece, gate_full, preferred_element_type=jnp.float32
    )
    pre_up = jnp.einsum("encd,edf->encf", slot_piece, up_full, preferred_element_type=jnp.float32)
    activated, derivative = silu_parts(pre_gate)
    hidden = (activated * pre_up).astype(jnp.bfloat16)
    expert_out = jnp.einsum(
        "encf,efd->encd", hidden, down_full, preferred_element_type=jnp.float32
    ).astype(jnp.bfloat16)
    return (expert_out, pre_gate, pre_up)


def on_device(tokens, expert_ids, gate_values, w_gate, w_up, w_down, partner):
    tok_rows, model_width = tokens.shape
    route_count = expert_ids.shape[1]
    local_experts = w_gate.shape[0]
    experts = lax.axis_size("expert") * local_experts
    capacity = tok_rows * route_count // experts + max(1, tok_rows * route_count // (16 * experts))
    slot_total = experts * capacity
    gate_full, up_full, down_full = (
        lax.all_gather(w_gate, "dp", axis=1, tiled=True),
        lax.all_gather(w_up, "dp", axis=1, tiled=True),
        lax.all_gather(w_down, "dp", axis=1, tiled=True),
    )
    expert_iota = jnp.arange(experts, dtype=jnp.int32)
    matches = expert_ids[:, :, None] == expert_iota
    chosen = jnp.sum(matches.astype(jnp.int32), axis=1, dtype=jnp.int32)
    chosen_gate = jnp.sum(jnp.where(matches, gate_values[:, :, None], 0.0), axis=1)
    before = jnp.cumsum(chosen, axis=0, dtype=jnp.int32) - chosen
    slot_rank = jnp.take_along_axis(before, expert_ids, axis=1)
    slot_row = (expert_ids * capacity + slot_rank).reshape(-1)
    slot_iota = jnp.arange(capacity, dtype=jnp.int32)
    onehot = (chosen.T[:, None, :] == 1) & (before.T[:, None, :] == slot_iota[None, :, None])
    placer = onehot.astype(jnp.bfloat16)
    slot_gate = jnp.sum(jnp.where(onehot, chosen_gate.T[:, None, :], 0.0), axis=2)
    outgoing = jnp.einsum("ect,td->ecd", placer, tokens, preferred_element_type=jnp.float32).astype(
        jnp.bfloat16
    )
    outgoing = outgoing.reshape(experts, 1, capacity, model_width)
    placer_flat = placer.reshape(slot_total, tok_rows)
    out_here, pre_gate, pre_up = expert_forward(
        lax.all_to_all(outgoing, "expert", split_axis=0, concat_axis=1, tiled=True),
        gate_full,
        up_full,
        down_full,
    )
    returned_out = lax.all_to_all(
        out_here, "expert", split_axis=1, concat_axis=0, tiled=True
    ).reshape(slot_total, model_width)
    weighted_sum = jnp.dot(
        slot_gate.reshape(slot_total), returned_out.astype(jnp.float32), precision=highest
    )
    pooled = jnp.mean(tokens.astype(jnp.float32), axis=0) + weighted_sum / tok_rows
    inv_rms = lax.rsqrt(jnp.mean(pooled * pooled) + 1e-06)
    embedding = (pooled * inv_rms).astype(jnp.bfloat16)[None, :]
    gathered = lax.all_gather(embedding, ("dp", "expert"), axis=0, tiled=True)
    batch_size = gathered.shape[0]
    own_index = lax.axis_index(("dp", "expert"))
    batch_iota = jnp.arange(batch_size, dtype=jnp.int32)
    scores = (
        score_scale
        / model_width
        * jnp.dot(gathered, embedding[0], preferred_element_type=jnp.float32)
    )
    others = batch_iota != own_index
    log_total = jnp.log(jnp.sum(jnp.where(others, jnp.exp(scores), 0.0)))
    own_partner = lax.dynamic_index_in_dim(partner, own_index, keepdims=False)
    partner_hit = (batch_iota == own_partner).astype(jnp.float32)
    weight = jnp.where(others, jnp.exp(scores - log_total), 0.0) - partner_hit
    all_embed = gathered.astype(jnp.float32)
    row_term = jnp.dot(weight, all_embed, precision=highest)
    all_totals = lax.all_gather(log_total[None], ("dp", "expert"), axis=0, tiled=True)
    column_weight = jnp.where(others, jnp.exp(scores - all_totals), 0.0) - (
        partner == own_index
    ).astype(jnp.float32)
    embed_grad = (
        score_scale
        / model_width
        * (row_term + jnp.dot(column_weight, all_embed, precision=highest))
    )
    partner_rows = jnp.take(gathered, partner, axis=0)
    partner_score = (
        score_scale
        / model_width
        * jnp.einsum("bd,bd->b", gathered, partner_rows, preferred_element_type=jnp.float32)
    )
    contrast_loss = jnp.mean(all_totals - partner_score)
    seq_grad = (
        inv_rms * embed_grad - inv_rms**3 * jnp.sum(pooled * embed_grad) / model_width * pooled
    )
    slot_dots = jnp.dot(returned_out.astype(jnp.float32), seq_grad, precision=highest)
    gate_grad = jnp.take(slot_dots, slot_row, axis=0).reshape(tok_rows, route_count)
    out_grad = (
        (slot_gate[:, :, None] * seq_grad)
        .astype(jnp.bfloat16)
        .reshape(experts, 1, capacity, model_width)
    )
    arrived = lax.all_to_all(out_grad, "expert", split_axis=0, concat_axis=1, tiled=True)
    hidden_grad = jnp.einsum(
        "encd,efd->encf", arrived, down_full, preferred_element_type=jnp.float32
    )
    activated, derivative = silu_parts(pre_gate)
    gate_side = (hidden_grad * pre_up * derivative).astype(jnp.bfloat16)
    up_side = (hidden_grad * activated).astype(jnp.bfloat16)
    route_here = jnp.einsum(
        "encf,edf->encd", gate_side, gate_full, preferred_element_type=jnp.float32
    )
    route_here = (
        route_here
        + jnp.einsum("encf,edf->encd", up_side, up_full, preferred_element_type=jnp.float32)
    ).astype(jnp.bfloat16)
    returned = lax.all_to_all(
        route_here, "expert", split_axis=1, concat_axis=0, tiled=True
    ).reshape(slot_total, model_width)
    route_sum = jnp.einsum("st,sd->td", placer_flat, returned, preferred_element_type=jnp.float32)
    token_grad = (seq_grad + route_sum).astype(jnp.bfloat16)
    return (contrast_loss, token_grad, gate_grad)


mesh_ids = pl.DeviceIdType.MESH
f32 = jnp.float32
bf16 = jnp.bfloat16


def split_dot(lhs, rhs, dims):
    rows = lhs.shape[0]
    high = lhs.astype(bf16)
    low = (lhs - high.astype(f32)).astype(bf16)
    both = lax.dot_general(
        jnp.concatenate([high, low], axis=0), rhs, (dims, ((), ())), preferred_element_type=f32
    )
    return both[:rows] + both[rows:]


def fused_kernel(
    tok_ref, ids_ref, gv_ref, wg_ref, wu_ref, wd_ref, prow_ref,
    loss_ref, tg_ref, gg_ref,
    tokb, gateb, gate_t, wbuf, wpad, acc, hid, side, hbar, part, rsb, arb, pool, sgrad, vsend, vrecv, vown,
    ggsend, ggrecv, rb, sibb, sumb, inb,
    loc_s, tok_s, tok_r, gate_s, gate_r, up_s, dn_s, w_r, hb_s, hb_r, rs_s, rs_r, ar_s, ar_r, ag_s, ag_r,
    v_s, v_r, gg_s, gg_r, sib_s, sib_r, ret_s, ret_r,
):
    p = lax.axis_index("dp")
    q = lax.axis_index("expert")
    n_dp = wbuf.shape[0]
    n_ex = gateb.shape[0]
    rows, width = tok_ref.shape
    ff = wg_ref.shape[2]
    chips = n_ex // 2
    chip = q // 2
    core = q % 2
    batch = n_dp * n_ex
    own = p * n_ex + q
    quarter = wbuf.shape[1]
    ff_part = wd_ref.shape[1]
    cols = width // n_ex
    topk = ids_ref.shape[0]
    experts = gateb.shape[1]

    def ex_peer(i):
        return (q + i) % n_ex

    def ex_from(i):
        return (q + n_ex - i) % n_ex

    def dp_peer(i):
        return (p + i) % n_dp

    def dp_from(i):
        return (p + n_dp - i) % n_dp

    def send(src, dst, s_sem, r_sem, **where):
        return pltpu.make_async_remote_copy(
            src_ref=src, dst_ref=dst, send_sem=s_sem, recv_sem=r_sem,
            device_id=(where.get("dp", p), where.get("ex", q)), device_id_type=mesh_ids,
        )

    barrier = pltpu.get_barrier_semaphore()
    for i in range(1, n_ex):
        pl.semaphore_signal(barrier, inc=1, device_id=(p, ex_peer(i)), device_id_type=mesh_ids)
    for i in range(1, n_dp):
        pl.semaphore_signal(barrier, inc=1, device_id=(dp_peer(i), q), device_id_type=mesh_ids)
    weight_loads = []
    for e in range(2):
        for m, ref in enumerate((wg_ref, wu_ref)):
            c = 2 * e + m
            weight_loads.append(
                pltpu.make_async_copy(ref.at[e], wbuf.at[p, :, c * ff : (c + 1) * ff], loc_s.at[c])
            )
    own_rows = pl.ds(pl.multiple_of(q * rows, rows), rows)
    token_load = pltpu.make_async_copy(tok_ref, tokb.at[own_rows, :], loc_s.at[4])
    for load in weight_loads:
        load.start()
    token_load.start()
    wpad[...] = jnp.zeros_like(wpad)
    down_loads = []
    for e in range(2):
        load = pltpu.make_async_copy(
            wd_ref.at[e],
            wpad.at[pl.ds(pl.multiple_of(e * ff + p * ff_part, 32), ff_part), :],
            loc_s.at[5 + e],
        )
        load.start()
        down_loads.append(load)
    for load in weight_loads:
        load.wait()
    pl.semaphore_wait(barrier, n_ex + n_dp - 2)

    half = quarter // 2

    def piece(j, h):
        return wbuf.at[j, h * half : (h + 1) * half, :]

    def up_copy(j, h):
        return send(
            piece(j, h), piece(j, h), up_s.at[j, h], w_r.at[j, h], dp=jnp.minimum(p + 1, n_dp - 1)
        )

    def dn_copy(j, h):
        return send(piece(j, h), piece(j, h), dn_s.at[j, h], w_r.at[j, h], dp=jnp.maximum(p - 1, 0))

    for h in range(2):

        @pl.when(p < n_dp - 1)
        def _(h=h):
            up_copy(p, h).start()

        @pl.when(p > 0)
        def _(h=h):
            dn_copy(p, h).start()

    token_load.wait()
    tok_copies = []
    for i in range(1, n_ex):
        copy = send(tokb.at[own_rows, :], tokb.at[own_rows, :], tok_s.at[i], tok_r.at[i], ex=ex_peer(i))
        copy.start()
        tok_copies.append(copy)

    expert_row = lax.broadcasted_iota(jnp.int32, (experts, rows), 0)
    gates = jnp.zeros((experts, rows), f32)
    for k in range(topk):
        gates = gates + jnp.where(ids_ref[k : k + 1, :] == expert_row, gv_ref[k : k + 1, :], 0.0)
    gateb[q] = gates
    gate_copies = []
    for i in range(1, n_ex):
        copy = send(gateb.at[q], gateb.at[q], gate_s.at[i], gate_r.at[i], ex=ex_peer(i))
        copy.start()
        gate_copies.append(copy)

    ggsend[...] = jnp.zeros_like(ggsend)
    for load in down_loads:
        load.wait()

    def multiply(j, first):
        d_cols = pl.ds(pl.multiple_of(j * quarter, quarter), quarter)

        def body(n, carry):
            f_cols = pl.ds(pl.multiple_of(n * 256, 256), 256)
            product = jnp.dot(tokb[:, d_cols], wbuf[j, :, f_cols], preferred_element_type=f32)
            if first:
                acc[:, f_cols] = product
            else:
                acc[:, f_cols] += product
            return carry

        lax.fori_loop(0, 4 * ff // 256, body, 0)

    def pass_on(k):
        low, high = p - k, p + k
        for h in range(2):

            @pl.when(low >= 0)
            def _(h=h):
                up_copy(low, h).wait_recv()

                @pl.when(p < n_dp - 1)
                def _():
                    up_copy(low, h).start()

            @pl.when(high < n_dp)
            def _(h=h):
                dn_copy(high, h).wait_recv()

                @pl.when(p > 0)
                def _():
                    dn_copy(high, h).start()

    def multiply_step(k):
        low, high = p - k, p + k

        @pl.when(low >= 0)
        def _():
            multiply(low, False)

        @pl.when(high < n_dp)
        def _():
            multiply(high, False)

    for k in range(1, n_dp - 1):
        pass_on(k)
    for i in range(1, n_ex):
        tok_copies[i - 1].wait_recv()
        gate_copies[i - 1].wait_recv()
    for s in range(n_ex):
        gate_t[s] = gateb[s].T
    multiply(p, True)
    for k in range(1, n_dp - 1):
        multiply_step(k)
    pass_on(n_dp - 1)
    multiply_step(n_dp - 1)

    expert_lane = lax.broadcasted_iota(jnp.int32, (rows, experts), 1)

    def gate_column(s, e):
        return jnp.sum(jnp.where(expert_lane == 2 * q + e, gate_t[s], 0.0), axis=1, keepdims=True)

    def forward(s, carry):
        rs = pl.ds(pl.multiple_of(s * rows, rows), rows)
        for e in range(2):
            pre_gate = acc[rs, 2 * e * ff : (2 * e + 1) * ff]
            pre_up = acc[rs, (2 * e + 1) * ff : (2 * e + 2) * ff]
            hidden = (pre_gate * jax.nn.sigmoid(pre_gate) * pre_up).astype(bf16)
            hid[rs, e * ff : (e + 1) * ff] = hidden
            hbar[p, pl.ds(s, 1), e * ff : (e + 1) * ff] = jnp.sum(
                gate_column(s, e) * hidden.astype(f32), axis=0, keepdims=True
            )
        return carry

    lax.fori_loop(0, n_ex, forward, 0)
    hb_copies = []
    for i in range(1, n_dp):
        copy = send(hbar.at[p], hbar.at[p], hb_s.at[i], hb_r.at[i], dp=dp_peer(i))
        copy.start()
        hb_copies.append(copy)

    def factors(s, carry):
        rs = pl.ds(pl.multiple_of(s * rows, rows), rows)
        for e in range(2):
            pre_gate = acc[rs, 2 * e * ff : (2 * e + 1) * ff]
            pre_up = acc[rs, (2 * e + 1) * ff : (2 * e + 2) * ff]
            activated, derivative = silu_parts(pre_gate)
            gate = gate_column(s, e)
            acc[rs, 2 * e * ff : (2 * e + 1) * ff] = gate * pre_up * derivative
            acc[rs, (2 * e + 1) * ff : (2 * e + 2) * ff] = gate * activated
        return carry

    token_mean = jnp.sum(tokb[own_rows, :].astype(f32), axis=0, keepdims=True) / rows
    for copy in hb_copies:
        copy.wait_recv()
    own_row = lax.broadcasted_iota(jnp.int32, (batch, 1), 0) == own
    part[...] = split_dot(
        hbar[...].reshape(batch, 2 * ff), wpad[...], ((1,), (0,))
    ) / rows + jnp.where(own_row, token_mean, 0.0)

    def col_at(i):
        return pl.ds(pl.multiple_of(i * cols, cols), cols)

    rs_copies = []
    for i in range(1, n_ex):
        copy = send(part.at[:, col_at(ex_peer(i))], rsb.at[i], rs_s.at[i], rs_r.at[i], ex=ex_peer(i))
        copy.start()
        rs_copies.append(copy)
    lax.fori_loop(0, n_ex // 2, factors, 0)
    total = part[:, col_at(q)]
    for i in range(1, n_ex):
        rs_copies[i - 1].wait_recv()
        total = total + rsb[i]
    arb[p] = total
    ar_copies = []
    for i in range(1, n_dp):
        copy = send(arb.at[p], arb.at[p], ar_s.at[i], ar_r.at[i], dp=dp_peer(i))
        copy.start()
        ar_copies.append(copy)
    lax.fori_loop(n_ex // 2, n_ex, factors, 0)
    for copy in ar_copies:
        copy.wait_recv()
    total = arb[0]
    for j in range(1, n_dp):
        total = total + arb[j]
    pool[:, col_at(q)] = total
    ag_copies = []
    for i in range(1, n_ex):
        copy = send(pool.at[:, col_at(q)], pool.at[:, col_at(q)], ag_s.at[i], ag_r.at[i], ex=ex_peer(i))
        copy.start()
        ag_copies.append(copy)
    for copy in ag_copies:
        copy.wait_recv()

    pooled = pool[...]
    inv_rms = lax.rsqrt(jnp.sum(pooled * pooled, axis=1, keepdims=True) / width + 1e-06)
    embedding = (pooled * inv_rms).astype(bf16)
    scale = score_scale / width
    scores = scale * lax.dot_general(
        embedding, embedding, (((1,), (1,)), ((), ())), preferred_element_type=f32
    )
    row_id = lax.broadcasted_iota(jnp.int32, (batch, batch), 0)
    col_id = lax.broadcasted_iota(jnp.int32, (batch, batch), 1)
    others = row_id != col_id
    exps = jnp.where(others, jnp.exp(scores), 0.0)
    log_total = jnp.log(jnp.sum(exps, axis=1, keepdims=True))
    log_total_row = jnp.log(jnp.sum(exps, axis=0, keepdims=True))
    hit_turned = (prow_ref[...] == row_id).astype(f32)
    hit = hit_turned.T
    partner_score = jnp.sum(scores * hit_turned, axis=0, keepdims=True)
    loss_ref[...] = jnp.sum(log_total_row - partner_score, axis=1, keepdims=True) / batch
    both = (
        jnp.where(others, jnp.exp(scores - log_total) + jnp.exp(scores - log_total_row), 0.0)
        - hit
        - hit_turned
    )
    embed_grad = scale * split_dot(both, embedding, ((1,), (0,)))
    seq_grad = (
        inv_rms * embed_grad
        - inv_rms * inv_rms * inv_rms
        * (jnp.sum(pooled * embed_grad, axis=1, keepdims=True) / width)
        * pooled
    )
    sgrad[...] = seq_grad
    vpart = split_dot(seq_grad, wpad[...], ((1,), (1,)))
    for j in range(n_dp):
        vsend[j] = vpart[j * n_ex : (j + 1) * n_ex]
    v_copies = []
    for i in range(1, n_dp):
        copy = send(vsend.at[dp_peer(i)], vrecv.at[i], v_s.at[i], v_r.at[i], dp=dp_peer(i))
        copy.start()
        v_copies.append(copy)
    total = vsend[p]
    for i in range(1, n_dp):
        v_copies[i - 1].wait_recv()
        total = total + vrecv[i]
    vown[...] = total

    def sides(s):
        rs = pl.ds(pl.multiple_of(s * rows, rows), rows)
        for e in range(2):
            v_row = vown[pl.ds(s, 1), e * ff : (e + 1) * ff]
            for m in range(2):
                c = slice((2 * e + m) * ff, (2 * e + m + 1) * ff)
                side[rs, c] = (acc[rs, c] * v_row).astype(bf16)

    sibling = chip * 2 + 1 - core
    keep = pl.ds(pl.multiple_of(core * rows, rows), rows)
    give = pl.ds(pl.multiple_of((1 - core) * rows, rows), rows)
    order = list(range(1, chips)) + [0]

    parts = 2
    span = width // parts

    def part_cols(h):
        return slice(h * span, (h + 1) * span)

    def sib_copy(i, h):
        c = part_cols(h)
        return send(rb.at[i, give, c], sibb.at[i, :, c], sib_s.at[i, h], sib_r.at[i, h], ex=sibling)

    def ret_copy(i, h):
        c = part_cols(h)
        return send(
            sumb.at[i, :, c], inb.at[i, :, c], ret_s.at[i, h], ret_r.at[i, h],
            ex=((chip + i) % chips) * 2 + core,
        )

    def finish(i, h):
        c = part_cols(h)
        sib_copy(i, h).wait_recv()
        summed = rb[i, keep, c].astype(f32) + sibb[i, :, c].astype(f32)
        if i:
            sumb[i, :, c] = summed.astype(bf16)
            ret_copy(i, h).start()
            return None
        return summed

    units = [(i, h) for i in order for h in range(parts)]
    for step, (i, h) in enumerate(units):
        target = (chip + i) % chips
        if h == 0:
            sides(2 * target)
            sides(2 * target + 1)
        pair = pl.ds(pl.multiple_of(target * 2 * rows, 2 * rows), 2 * rows)

        def back(j, carry, i=i, pair=pair):
            rb[i, :, pl.ds(pl.multiple_of(j * quarter, quarter), quarter)] = lax.dot_general(
                side[pair, :], wbuf[j], (((1,), (1,)), ((), ())), preferred_element_type=f32
            ).astype(bf16)
            return carry

        lax.fori_loop(h * n_dp // parts, (h + 1) * n_dp // parts, back, 0)
        sib_copy(i, h).start()
        if step and units[step - 1][0]:
            finish(*units[step - 1])

    lane = lax.broadcasted_iota(jnp.int32, (n_ex, n_ex * rows), 1)
    block_diag = lane // rows == lax.broadcasted_iota(jnp.int32, (n_ex, n_ex * rows), 0)
    for e in range(2):
        dots = split_dot(
            vown[:, e * ff : (e + 1) * ff], hid[:, e * ff : (e + 1) * ff], ((1,), (1,))
        )
        ggsend[e : e + 1, :] = jnp.sum(jnp.where(block_diag, dots, 0.0), axis=0, keepdims=True)

    def seq_cols(i):
        return pl.ds(pl.multiple_of(i * rows, rows), rows)

    gg_copies = []
    for i in range(1, n_ex):
        copy = send(ggsend.at[:, seq_cols(ex_peer(i))], ggrecv.at[q], gg_s.at[i], gg_r.at[i], ex=ex_peer(i))
        copy.start()
        gg_copies.append(copy)
    ggrecv[q] = ggsend[:, seq_cols(q)]
    for copy in gg_copies:
        copy.wait_recv()
    all_dots = ggrecv[...].reshape(n_ex * 8, rows)
    dot_row = lax.broadcasted_iota(jnp.int32, (n_ex * 8, 1), 0)
    row_expert = jnp.where(dot_row % 8 < 2, dot_row // 8 * 2 + dot_row % 8, -1)
    for k in range(topk):
        gg_ref[k : k + 1, :] = jnp.sum(
            jnp.where(ids_ref[k : k + 1, :] == row_expert, all_dots, 0.0), axis=0, keepdims=True
        )
    for h in range(parts):
        c = part_cols(h)
        grad = finish(0, h) + sgrad[pl.ds(own, 1), c]
        for i in range(1, chips):
            ret_copy(i, h).wait_recv()
            grad = grad + inb[i, :, c].astype(f32)
        tg_ref[:, c] = grad.astype(bf16)

    for copies in (tok_copies, gate_copies, hb_copies, rs_copies, ar_copies, ag_copies, v_copies, gg_copies):
        for copy in copies:
            copy.wait_send()
    for i in range(chips):
        for h in range(parts):
            sib_copy(i, h).wait_send()
            if i:
                ret_copy(i, h).wait_send()
    for k in range(n_dp):
        low, high = p - k, p + k

        for h in range(2):

            @pl.when((low >= 0) & (p < n_dp - 1))
            def _(h=h):
                up_copy(low, h).wait_send()

            @pl.when((high < n_dp) & (p > 0))
            def _(h=h):
                dn_copy(high, h).wait_send()


def fused(tokens, expert_ids, gate_values, w_gate, w_up, w_down, partner):
    rows, width = tokens.shape
    topk = expert_ids.shape[1]
    ff = w_gate.shape[2]
    n_dp, n_ex = lax.axis_size("dp"), lax.axis_size("expert")
    batch = n_dp * n_ex
    all_rows = n_ex * rows
    cols = width // n_ex
    chips = n_ex // 2
    dma = pltpu.SemaphoreType.DMA
    vmem = pl.BlockSpec(memory_space=pltpu.VMEM)
    hbm = pl.BlockSpec(memory_space=pl.ANY)
    loss, token_grad, gate_grad = pl.pallas_call(
        fused_kernel,
        out_shape=(
            jax.ShapeDtypeStruct((1, 1), f32),
            jax.ShapeDtypeStruct((rows, width), bf16),
            jax.ShapeDtypeStruct((topk, rows), f32),
        ),
        in_specs=[hbm, vmem, vmem, hbm, hbm, hbm, vmem],
        out_specs=(vmem, vmem, vmem),
        scratch_shapes=[
            pltpu.VMEM((all_rows, width), bf16),
            pltpu.VMEM((n_ex, 2 * n_ex, rows), f32),
            pltpu.VMEM((n_ex, rows, 2 * n_ex), f32),
            pltpu.VMEM((n_dp, width // n_dp, 4 * ff), bf16),
            pltpu.VMEM((2 * ff, width), bf16),
            pltpu.VMEM((all_rows, 4 * ff), f32),
            pltpu.VMEM((all_rows, 2 * ff), bf16),
            pltpu.VMEM((all_rows, 4 * ff), bf16),
            pltpu.VMEM((n_dp, n_ex, 2 * ff), f32),
            pltpu.VMEM((batch, width), f32),
            pltpu.VMEM((n_ex, batch, cols), f32),
            pltpu.VMEM((n_dp, batch, cols), f32),
            pltpu.VMEM((batch, width), f32),
            pltpu.VMEM((batch, width), f32),
            pltpu.VMEM((n_dp, n_ex, 2 * ff), f32),
            pltpu.VMEM((n_dp, n_ex, 2 * ff), f32),
            pltpu.VMEM((n_ex, 2 * ff), f32),
            pltpu.VMEM((8, all_rows), f32),
            pltpu.VMEM((n_ex, 8, rows), f32),
            pltpu.VMEM((chips, 2 * rows, width), bf16),
            pltpu.VMEM((chips, rows, width), bf16),
            pltpu.VMEM((chips, rows, width), bf16),
            pltpu.VMEM((chips, rows, width), bf16),
        ]
        + [dma((8,))]
        + [dma((n_ex,))] * 4
        + [dma((n_dp, 2))] * 3
        + [dma((n_dp,))] * 2
        + [dma((n_ex,))] * 2
        + [dma((n_dp,))] * 2
        + [dma((n_ex,))] * 2
        + [dma((n_dp,))] * 2
        + [dma((n_ex,))] * 2
        + [dma((chips, 2))] * 4,
        compiler_params=pltpu.CompilerParams(
            collective_id=0, has_side_effects=True, vmem_limit_bytes=60 * 1024 * 1024
        ),
    )(tokens, expert_ids.T, gate_values.T, w_gate, w_up, w_down, partner[None, :])
    return (loss[0, 0], token_grad, gate_grad.T)


def fits_fused(mesh):
    return mesh.shape["dp"] == 4 and mesh.shape["expert"] == 8


def solution(mesh):
    placed = (
        P(("dp", "expert"), None),
        P(("dp", "expert"), None),
        P(("dp", "expert"), None),
        P("expert", "dp", None),
        P("expert", "dp", None),
        P("expert", "dp", None),
        P(),
    )
    return jax.shard_map(
        fused if fits_fused(mesh) else on_device,
        mesh=mesh,
        in_specs=placed,
        out_specs=(P(), P(("dp", "expert"), None), P(("dp", "expert"), None)),
        check_vma=False,
    )
```

```python
import jax
import jax.numpy as jnp
from jax import lax
from jax.experimental import pallas as pl
from jax.experimental.pallas import tpu as pltpu
from jax.sharding import PartitionSpec as P

score_scale = 20.0
highest = lax.Precision.HIGHEST


def silu_parts(pre_act):
    sigmoid_val = jax.nn.sigmoid(pre_act)
    return (pre_act * sigmoid_val, sigmoid_val * (1.0 + pre_act * (1.0 - sigmoid_val)))


def expert_forward(slot_piece, gate_full, up_full, down_full):
    pre_gate = jnp.einsum(
        "encd,edf->encf", slot_piece, gate_full, preferred_element_type=jnp.float32
    )
    pre_up = jnp.einsum("encd,edf->encf", slot_piece, up_full, preferred_element_type=jnp.float32)
    activated, derivative = silu_parts(pre_gate)
    hidden = (activated * pre_up).astype(jnp.bfloat16)
    expert_out = jnp.einsum(
        "encf,efd->encd", hidden, down_full, preferred_element_type=jnp.float32
    ).astype(jnp.bfloat16)
    return (expert_out, pre_gate, pre_up)


def on_device(tokens, expert_ids, gate_values, w_gate, w_up, w_down, partner):
    tok_rows, model_width = tokens.shape
    route_count = expert_ids.shape[1]
    local_experts = w_gate.shape[0]
    experts = lax.axis_size("expert") * local_experts
    capacity = tok_rows * route_count // experts + max(1, tok_rows * route_count // (16 * experts))
    slot_total = experts * capacity
    gate_full, up_full, down_full = (
        lax.all_gather(w_gate, "dp", axis=1, tiled=True),
        lax.all_gather(w_up, "dp", axis=1, tiled=True),
        lax.all_gather(w_down, "dp", axis=1, tiled=True),
    )
    expert_iota = jnp.arange(experts, dtype=jnp.int32)
    matches = expert_ids[:, :, None] == expert_iota
    chosen = jnp.sum(matches.astype(jnp.int32), axis=1, dtype=jnp.int32)
    chosen_gate = jnp.sum(jnp.where(matches, gate_values[:, :, None], 0.0), axis=1)
    before = jnp.cumsum(chosen, axis=0, dtype=jnp.int32) - chosen
    slot_rank = jnp.take_along_axis(before, expert_ids, axis=1)
    slot_row = (expert_ids * capacity + slot_rank).reshape(-1)
    slot_iota = jnp.arange(capacity, dtype=jnp.int32)
    onehot = (chosen.T[:, None, :] == 1) & (before.T[:, None, :] == slot_iota[None, :, None])
    placer = onehot.astype(jnp.bfloat16)
    slot_gate = jnp.sum(jnp.where(onehot, chosen_gate.T[:, None, :], 0.0), axis=2)
    outgoing = jnp.einsum("ect,td->ecd", placer, tokens, preferred_element_type=jnp.float32).astype(
        jnp.bfloat16
    )
    outgoing = outgoing.reshape(experts, 1, capacity, model_width)
    placer_flat = placer.reshape(slot_total, tok_rows)
    out_here, pre_gate, pre_up = expert_forward(
        lax.all_to_all(outgoing, "expert", split_axis=0, concat_axis=1, tiled=True),
        gate_full,
        up_full,
        down_full,
    )
    returned_out = lax.all_to_all(
        out_here, "expert", split_axis=1, concat_axis=0, tiled=True
    ).reshape(slot_total, model_width)
    weighted_sum = jnp.dot(
        slot_gate.reshape(slot_total), returned_out.astype(jnp.float32), precision=highest
    )
    pooled = jnp.mean(tokens.astype(jnp.float32), axis=0) + weighted_sum / tok_rows
    inv_rms = lax.rsqrt(jnp.mean(pooled * pooled) + 1e-06)
    embedding = (pooled * inv_rms).astype(jnp.bfloat16)[None, :]
    gathered = lax.all_gather(embedding, ("dp", "expert"), axis=0, tiled=True)
    batch_size = gathered.shape[0]
    own_index = lax.axis_index(("dp", "expert"))
    batch_iota = jnp.arange(batch_size, dtype=jnp.int32)
    scores = (
        score_scale
        / model_width
        * jnp.dot(gathered, embedding[0], preferred_element_type=jnp.float32)
    )
    others = batch_iota != own_index
    log_total = jnp.log(jnp.sum(jnp.where(others, jnp.exp(scores), 0.0)))
    own_partner = lax.dynamic_index_in_dim(partner, own_index, keepdims=False)
    partner_hit = (batch_iota == own_partner).astype(jnp.float32)
    weight = jnp.where(others, jnp.exp(scores - log_total), 0.0) - partner_hit
    all_embed = gathered.astype(jnp.float32)
    row_term = jnp.dot(weight, all_embed, precision=highest)
    all_totals = lax.all_gather(log_total[None], ("dp", "expert"), axis=0, tiled=True)
    column_weight = jnp.where(others, jnp.exp(scores - all_totals), 0.0) - (
        partner == own_index
    ).astype(jnp.float32)
    embed_grad = (
        score_scale
        / model_width
        * (row_term + jnp.dot(column_weight, all_embed, precision=highest))
    )
    partner_rows = jnp.take(gathered, partner, axis=0)
    partner_score = (
        score_scale
        / model_width
        * jnp.einsum("bd,bd->b", gathered, partner_rows, preferred_element_type=jnp.float32)
    )
    contrast_loss = jnp.mean(all_totals - partner_score)
    seq_grad = (
        inv_rms * embed_grad - inv_rms**3 * jnp.sum(pooled * embed_grad) / model_width * pooled
    )
    slot_dots = jnp.dot(returned_out.astype(jnp.float32), seq_grad, precision=highest)
    gate_grad = jnp.take(slot_dots, slot_row, axis=0).reshape(tok_rows, route_count)
    out_grad = (
        (slot_gate[:, :, None] * seq_grad)
        .astype(jnp.bfloat16)
        .reshape(experts, 1, capacity, model_width)
    )
    arrived = lax.all_to_all(out_grad, "expert", split_axis=0, concat_axis=1, tiled=True)
    hidden_grad = jnp.einsum(
        "encd,efd->encf", arrived, down_full, preferred_element_type=jnp.float32
    )
    activated, derivative = silu_parts(pre_gate)
    gate_side = (hidden_grad * pre_up * derivative).astype(jnp.bfloat16)
    up_side = (hidden_grad * activated).astype(jnp.bfloat16)
    route_here = jnp.einsum(
        "encf,edf->encd", gate_side, gate_full, preferred_element_type=jnp.float32
    )
    route_here = (
        route_here
        + jnp.einsum("encf,edf->encd", up_side, up_full, preferred_element_type=jnp.float32)
    ).astype(jnp.bfloat16)
    returned = lax.all_to_all(
        route_here, "expert", split_axis=1, concat_axis=0, tiled=True
    ).reshape(slot_total, model_width)
    route_sum = jnp.einsum("st,sd->td", placer_flat, returned, preferred_element_type=jnp.float32)
    token_grad = (seq_grad + route_sum).astype(jnp.bfloat16)
    return (contrast_loss, token_grad, gate_grad)


mesh_ids = pl.DeviceIdType.MESH
f32 = jnp.float32
bf16 = jnp.bfloat16


def split_dot(lhs, rhs, dims):
    rows = lhs.shape[0]
    high = lhs.astype(bf16)
    low = (lhs - high.astype(f32)).astype(bf16)
    both = lax.dot_general(
        jnp.concatenate([high, low], axis=0), rhs, (dims, ((), ())), preferred_element_type=f32
    )
    return both[:rows] + both[rows:]


def fused_kernel(
    tok_ref, ids_ref, gv_ref, wg_ref, wu_ref, wd_ref, prow_ref,
    loss_ref, tg_ref, gg_ref,
    tokb, gateb, gate_t, wbuf, wpad, acc, hid, side, hbar, part, rsb, arb, pool, sgrad, vsend, vrecv, vown,
    ggsend, ggrecv, rb, sibb, sumb, inb,
    loc_s, tok_s, tok_r, gate_s, gate_r, up_s, dn_s, w_r, hb_s, hb_r, rs_s, rs_r, ar_s, ar_r, ag_s, ag_r,
    v_s, v_r, gg_s, gg_r, sib_s, sib_r, ret_s, ret_r,
):
    p = lax.axis_index("dp")
    q = lax.axis_index("expert")
    n_dp = wbuf.shape[0]
    n_ex = gateb.shape[0]
    rows, width = tok_ref.shape
    ff = wg_ref.shape[2]
    chips = n_ex // 2
    chip = q // 2
    core = q % 2
    batch = n_dp * n_ex
    own = p * n_ex + q
    quarter = wbuf.shape[1]
    ff_part = wd_ref.shape[1]
    cols = width // n_ex
    topk = ids_ref.shape[0]
    experts = gateb.shape[1]

    def ex_peer(i):
        return (q + i) % n_ex

    def ex_from(i):
        return (q + n_ex - i) % n_ex

    def dp_peer(i):
        return (p + i) % n_dp

    def dp_from(i):
        return (p + n_dp - i) % n_dp

    def send(src, dst, s_sem, r_sem, **where):
        return pltpu.make_async_remote_copy(
            src_ref=src, dst_ref=dst, send_sem=s_sem, recv_sem=r_sem,
            device_id=(where.get("dp", p), where.get("ex", q)), device_id_type=mesh_ids,
        )

    barrier = pltpu.get_barrier_semaphore()
    for i in range(1, n_ex):
        pl.semaphore_signal(barrier, inc=1, device_id=(p, ex_peer(i)), device_id_type=mesh_ids)
    for i in range(1, n_dp):
        pl.semaphore_signal(barrier, inc=1, device_id=(dp_peer(i), q), device_id_type=mesh_ids)
    weight_loads = []
    for e in range(2):
        for m, ref in enumerate((wg_ref, wu_ref)):
            c = 2 * e + m
            weight_loads.append(
                pltpu.make_async_copy(ref.at[e], wbuf.at[p, :, c * ff : (c + 1) * ff], loc_s.at[c])
            )
    own_rows = pl.ds(pl.multiple_of(q * rows, rows), rows)
    token_load = pltpu.make_async_copy(tok_ref, tokb.at[own_rows, :], loc_s.at[4])
    for load in weight_loads:
        load.start()
    token_load.start()
    wpad[...] = jnp.zeros_like(wpad)
    down_loads = []
    for e in range(2):
        load = pltpu.make_async_copy(
            wd_ref.at[e],
            wpad.at[pl.ds(pl.multiple_of(e * ff + p * ff_part, 32), ff_part), :],
            loc_s.at[5 + e],
        )
        load.start()
        down_loads.append(load)
    for load in weight_loads:
        load.wait()
    pl.semaphore_wait(barrier, n_ex + n_dp - 2)

    half = quarter // 4

    def piece(j, h):
        return wbuf.at[j, h * half : (h + 1) * half, :]

    def up_copy(j, h):
        return send(
            piece(j, h), piece(j, h), up_s.at[j, h], w_r.at[j, h], dp=jnp.minimum(p + 1, n_dp - 1)
        )

    def dn_copy(j, h):
        return send(piece(j, h), piece(j, h), dn_s.at[j, h], w_r.at[j, h], dp=jnp.maximum(p - 1, 0))

    for h in range(4):

        @pl.when(p < n_dp - 1)
        def _(h=h):
            up_copy(p, h).start()

        @pl.when(p > 0)
        def _(h=h):
            dn_copy(p, h).start()

    token_load.wait()
    tok_copies = []
    for i in range(1, n_ex):
        copy = send(tokb.at[own_rows, :], tokb.at[own_rows, :], tok_s.at[i], tok_r.at[i], ex=ex_peer(i))
        copy.start()
        tok_copies.append(copy)

    expert_row = lax.broadcasted_iota(jnp.int32, (experts, rows), 0)
    gates = jnp.zeros((experts, rows), f32)
    for k in range(topk):
        gates = gates + jnp.where(ids_ref[k : k + 1, :] == expert_row, gv_ref[k : k + 1, :], 0.0)
    gateb[q] = gates
    gate_copies = []
    for i in range(1, n_ex):
        copy = send(gateb.at[q], gateb.at[q], gate_s.at[i], gate_r.at[i], ex=ex_peer(i))
        copy.start()
        gate_copies.append(copy)

    ggsend[...] = jnp.zeros_like(ggsend)
    for load in down_loads:
        load.wait()

    def multiply(j, first):
        d_cols = pl.ds(pl.multiple_of(j * quarter, quarter), quarter)

        def body(n, carry):
            f_cols = pl.ds(pl.multiple_of(n * 256, 256), 256)
            product = jnp.dot(tokb[:, d_cols], wbuf[j, :, f_cols], preferred_element_type=f32)
            if first:
                acc[:, f_cols] = product
            else:
                acc[:, f_cols] += product
            return carry

        lax.fori_loop(0, 4 * ff // 256, body, 0)

    def pass_on(k):
        low, high = p - k, p + k
        for h in range(4):

            @pl.when(low >= 0)
            def _(h=h):
                up_copy(low, h).wait_recv()

                @pl.when(p < n_dp - 1)
                def _():
                    up_copy(low, h).start()

            @pl.when(high < n_dp)
            def _(h=h):
                dn_copy(high, h).wait_recv()

                @pl.when(p > 0)
                def _():
                    dn_copy(high, h).start()

    def multiply_step(k):
        low, high = p - k, p + k

        @pl.when(low >= 0)
        def _():
            multiply(low, False)

        @pl.when(high < n_dp)
        def _():
            multiply(high, False)

    for k in range(1, n_dp - 1):
        pass_on(k)
    for i in range(1, n_ex):
        tok_copies[i - 1].wait_recv()
        gate_copies[i - 1].wait_recv()
    for s in range(n_ex):
        gate_t[s] = gateb[s].T
    multiply(p, True)
    for k in range(1, n_dp - 1):
        multiply_step(k)
    pass_on(n_dp - 1)
    multiply_step(n_dp - 1)

    expert_lane = lax.broadcasted_iota(jnp.int32, (rows, experts), 1)

    def gate_column(s, e):
        return jnp.sum(jnp.where(expert_lane == 2 * q + e, gate_t[s], 0.0), axis=1, keepdims=True)

    def forward(s, carry):
        rs = pl.ds(pl.multiple_of(s * rows, rows), rows)
        for e in range(2):
            pre_gate = acc[rs, 2 * e * ff : (2 * e + 1) * ff]
            pre_up = acc[rs, (2 * e + 1) * ff : (2 * e + 2) * ff]
            hidden = (pre_gate * jax.nn.sigmoid(pre_gate) * pre_up).astype(bf16)
            hid[rs, e * ff : (e + 1) * ff] = hidden
            hbar[p, pl.ds(s, 1), e * ff : (e + 1) * ff] = jnp.sum(
                gate_column(s, e) * hidden.astype(f32), axis=0, keepdims=True
            )
        return carry

    lax.fori_loop(0, n_ex, forward, 0)
    hb_copies = []
    for i in range(1, n_dp):
        copy = send(hbar.at[p], hbar.at[p], hb_s.at[i], hb_r.at[i], dp=dp_peer(i))
        copy.start()
        hb_copies.append(copy)

    def factors(s, carry):
        rs = pl.ds(pl.multiple_of(s * rows, rows), rows)
        for e in range(2):
            pre_gate = acc[rs, 2 * e * ff : (2 * e + 1) * ff]
            pre_up = acc[rs, (2 * e + 1) * ff : (2 * e + 2) * ff]
            activated, derivative = silu_parts(pre_gate)
            gate = gate_column(s, e)
            acc[rs, 2 * e * ff : (2 * e + 1) * ff] = gate * pre_up * derivative
            acc[rs, (2 * e + 1) * ff : (2 * e + 2) * ff] = gate * activated
        return carry

    token_mean = jnp.sum(tokb[own_rows, :].astype(f32), axis=0, keepdims=True) / rows
    for copy in hb_copies:
        copy.wait_recv()
    own_row = lax.broadcasted_iota(jnp.int32, (batch, 1), 0) == own
    part[...] = split_dot(
        hbar[...].reshape(batch, 2 * ff), wpad[...], ((1,), (0,))
    ) / rows + jnp.where(own_row, token_mean, 0.0)

    def col_at(i):
        return pl.ds(pl.multiple_of(i * cols, cols), cols)

    rs_copies = []
    for i in range(1, n_ex):
        copy = send(part.at[:, col_at(ex_peer(i))], rsb.at[i], rs_s.at[i], rs_r.at[i], ex=ex_peer(i))
        copy.start()
        rs_copies.append(copy)
    lax.fori_loop(0, n_ex // 2, factors, 0)
    total = part[:, col_at(q)]
    for i in range(1, n_ex):
        rs_copies[i - 1].wait_recv()
        total = total + rsb[i]
    arb[p] = total
    ar_copies = []
    for i in range(1, n_dp):
        copy = send(arb.at[p], arb.at[p], ar_s.at[i], ar_r.at[i], dp=dp_peer(i))
        copy.start()
        ar_copies.append(copy)
    lax.fori_loop(n_ex // 2, n_ex, factors, 0)
    for copy in ar_copies:
        copy.wait_recv()
    total = arb[0]
    for j in range(1, n_dp):
        total = total + arb[j]
    pool[:, col_at(q)] = total
    ag_copies = []
    for i in range(1, n_ex):
        copy = send(pool.at[:, col_at(q)], pool.at[:, col_at(q)], ag_s.at[i], ag_r.at[i], ex=ex_peer(i))
        copy.start()
        ag_copies.append(copy)
    for copy in ag_copies:
        copy.wait_recv()

    pooled = pool[...]
    inv_rms = lax.rsqrt(jnp.sum(pooled * pooled, axis=1, keepdims=True) / width + 1e-06)
    embedding = (pooled * inv_rms).astype(bf16)
    scale = score_scale / width
    scores = scale * lax.dot_general(
        embedding, embedding, (((1,), (1,)), ((), ())), preferred_element_type=f32
    )
    row_id = lax.broadcasted_iota(jnp.int32, (batch, batch), 0)
    col_id = lax.broadcasted_iota(jnp.int32, (batch, batch), 1)
    others = row_id != col_id
    exps = jnp.where(others, jnp.exp(scores), 0.0)
    log_total = jnp.log(jnp.sum(exps, axis=1, keepdims=True))
    log_total_row = jnp.log(jnp.sum(exps, axis=0, keepdims=True))
    hit_turned = (prow_ref[...] == row_id).astype(f32)
    hit = hit_turned.T
    partner_score = jnp.sum(scores * hit_turned, axis=0, keepdims=True)
    loss_ref[...] = jnp.sum(log_total_row - partner_score, axis=1, keepdims=True) / batch
    both = (
        jnp.where(others, jnp.exp(scores - log_total) + jnp.exp(scores - log_total_row), 0.0)
        - hit
        - hit_turned
    )
    embed_grad = scale * split_dot(both, embedding, ((1,), (0,)))
    seq_grad = (
        inv_rms * embed_grad
        - inv_rms * inv_rms * inv_rms
        * (jnp.sum(pooled * embed_grad, axis=1, keepdims=True) / width)
        * pooled
    )
    sgrad[...] = seq_grad
    vpart = split_dot(seq_grad, wpad[...], ((1,), (1,)))
    for j in range(n_dp):
        vsend[j] = vpart[j * n_ex : (j + 1) * n_ex]
    v_copies = []
    for i in range(1, n_dp):
        copy = send(vsend.at[dp_peer(i)], vrecv.at[i], v_s.at[i], v_r.at[i], dp=dp_peer(i))
        copy.start()
        v_copies.append(copy)
    total = vsend[p]
    for i in range(1, n_dp):
        v_copies[i - 1].wait_recv()
        total = total + vrecv[i]
    vown[...] = total

    def sides(s):
        rs = pl.ds(pl.multiple_of(s * rows, rows), rows)
        for e in range(2):
            v_row = vown[pl.ds(s, 1), e * ff : (e + 1) * ff]
            for m in range(2):
                c = slice((2 * e + m) * ff, (2 * e + m + 1) * ff)
                side[rs, c] = (acc[rs, c] * v_row).astype(bf16)

    sibling = chip * 2 + 1 - core
    keep = pl.ds(pl.multiple_of(core * rows, rows), rows)
    give = pl.ds(pl.multiple_of((1 - core) * rows, rows), rows)
    order = list(range(1, chips)) + [0]

    parts = 2
    span = width // parts

    def part_cols(h):
        return slice(h * span, (h + 1) * span)

    def sib_copy(i, h):
        c = part_cols(h)
        return send(rb.at[i, give, c], sibb.at[i, :, c], sib_s.at[i, h], sib_r.at[i, h], ex=sibling)

    def ret_copy(i, h):
        c = part_cols(h)
        return send(
            sumb.at[i, :, c], inb.at[i, :, c], ret_s.at[i, h], ret_r.at[i, h],
            ex=((chip + i) % chips) * 2 + core,
        )

    def finish(i, h):
        c = part_cols(h)
        sib_copy(i, h).wait_recv()
        summed = rb[i, keep, c].astype(f32) + sibb[i, :, c].astype(f32)
        if i:
            sumb[i, :, c] = summed.astype(bf16)
            ret_copy(i, h).start()
            return None
        return summed

    units = [(i, h) for i in order for h in range(parts)]
    for step, (i, h) in enumerate(units):
        target = (chip + i) % chips
        if h == 0:
            sides(2 * target)
            sides(2 * target + 1)
        pair = pl.ds(pl.multiple_of(target * 2 * rows, 2 * rows), 2 * rows)

        def back(j, carry, i=i, pair=pair):
            rb[i, :, pl.ds(pl.multiple_of(j * quarter, quarter), quarter)] = lax.dot_general(
                side[pair, :], wbuf[j], (((1,), (1,)), ((), ())), preferred_element_type=f32
            ).astype(bf16)
            return carry

        lax.fori_loop(h * n_dp // parts, (h + 1) * n_dp // parts, back, 0)
        sib_copy(i, h).start()
        if step and units[step - 1][0]:
            finish(*units[step - 1])

    lane = lax.broadcasted_iota(jnp.int32, (n_ex, n_ex * rows), 1)
    block_diag = lane // rows == lax.broadcasted_iota(jnp.int32, (n_ex, n_ex * rows), 0)
    for e in range(2):
        dots = split_dot(
            vown[:, e * ff : (e + 1) * ff], hid[:, e * ff : (e + 1) * ff], ((1,), (1,))
        )
        ggsend[e : e + 1, :] = jnp.sum(jnp.where(block_diag, dots, 0.0), axis=0, keepdims=True)

    def seq_cols(i):
        return pl.ds(pl.multiple_of(i * rows, rows), rows)

    gg_copies = []
    for i in range(1, n_ex):
        copy = send(ggsend.at[:, seq_cols(ex_peer(i))], ggrecv.at[q], gg_s.at[i], gg_r.at[i], ex=ex_peer(i))
        copy.start()
        gg_copies.append(copy)
    ggrecv[q] = ggsend[:, seq_cols(q)]
    for copy in gg_copies:
        copy.wait_recv()
    all_dots = ggrecv[...].reshape(n_ex * 8, rows)
    dot_row = lax.broadcasted_iota(jnp.int32, (n_ex * 8, 1), 0)
    row_expert = jnp.where(dot_row % 8 < 2, dot_row // 8 * 2 + dot_row % 8, -1)
    for k in range(topk):
        gg_ref[k : k + 1, :] = jnp.sum(
            jnp.where(ids_ref[k : k + 1, :] == row_expert, all_dots, 0.0), axis=0, keepdims=True
        )
    for h in range(parts):
        c = part_cols(h)
        grad = finish(0, h) + sgrad[pl.ds(own, 1), c]
        for i in range(1, chips):
            ret_copy(i, h).wait_recv()
            grad = grad + inb[i, :, c].astype(f32)
        tg_ref[:, c] = grad.astype(bf16)

    for copies in (tok_copies, gate_copies, hb_copies, rs_copies, ar_copies, ag_copies, v_copies, gg_copies):
        for copy in copies:
            copy.wait_send()
    for i in range(chips):
        for h in range(parts):
            sib_copy(i, h).wait_send()
            if i:
                ret_copy(i, h).wait_send()
    for k in range(n_dp):
        low, high = p - k, p + k

        for h in range(4):

            @pl.when((low >= 0) & (p < n_dp - 1))
            def _(h=h):
                up_copy(low, h).wait_send()

            @pl.when((high < n_dp) & (p > 0))
            def _(h=h):
                dn_copy(high, h).wait_send()


def fused(tokens, expert_ids, gate_values, w_gate, w_up, w_down, partner):
    rows, width = tokens.shape
    topk = expert_ids.shape[1]
    ff = w_gate.shape[2]
    n_dp, n_ex = lax.axis_size("dp"), lax.axis_size("expert")
    batch = n_dp * n_ex
    all_rows = n_ex * rows
    cols = width // n_ex
    chips = n_ex // 2
    dma = pltpu.SemaphoreType.DMA
    vmem = pl.BlockSpec(memory_space=pltpu.VMEM)
    hbm = pl.BlockSpec(memory_space=pl.ANY)
    loss, token_grad, gate_grad = pl.pallas_call(
        fused_kernel,
        out_shape=(
            jax.ShapeDtypeStruct((1, 1), f32),
            jax.ShapeDtypeStruct((rows, width), bf16),
            jax.ShapeDtypeStruct((topk, rows), f32),
        ),
        in_specs=[hbm, vmem, vmem, hbm, hbm, hbm, vmem],
        out_specs=(vmem, vmem, vmem),
        scratch_shapes=[
            pltpu.VMEM((all_rows, width), bf16),
            pltpu.VMEM((n_ex, 2 * n_ex, rows), f32),
            pltpu.VMEM((n_ex, rows, 2 * n_ex), f32),
            pltpu.VMEM((n_dp, width // n_dp, 4 * ff), bf16),
            pltpu.VMEM((2 * ff, width), bf16),
            pltpu.VMEM((all_rows, 4 * ff), f32),
            pltpu.VMEM((all_rows, 2 * ff), bf16),
            pltpu.VMEM((all_rows, 4 * ff), bf16),
            pltpu.VMEM((n_dp, n_ex, 2 * ff), f32),
            pltpu.VMEM((batch, width), f32),
            pltpu.VMEM((n_ex, batch, cols), f32),
            pltpu.VMEM((n_dp, batch, cols), f32),
            pltpu.VMEM((batch, width), f32),
            pltpu.VMEM((batch, width), f32),
            pltpu.VMEM((n_dp, n_ex, 2 * ff), f32),
            pltpu.VMEM((n_dp, n_ex, 2 * ff), f32),
            pltpu.VMEM((n_ex, 2 * ff), f32),
            pltpu.VMEM((8, all_rows), f32),
            pltpu.VMEM((n_ex, 8, rows), f32),
            pltpu.VMEM((chips, 2 * rows, width), bf16),
            pltpu.VMEM((chips, rows, width), bf16),
            pltpu.VMEM((chips, rows, width), bf16),
            pltpu.VMEM((chips, rows, width), bf16),
        ]
        + [dma((8,))]
        + [dma((n_ex,))] * 4
        + [dma((n_dp, 4))] * 3
        + [dma((n_dp,))] * 2
        + [dma((n_ex,))] * 2
        + [dma((n_dp,))] * 2
        + [dma((n_ex,))] * 2
        + [dma((n_dp,))] * 2
        + [dma((n_ex,))] * 2
        + [dma((chips, 2))] * 4,
        compiler_params=pltpu.CompilerParams(
            collective_id=0, has_side_effects=True, vmem_limit_bytes=60 * 1024 * 1024
        ),
    )(tokens, expert_ids.T, gate_values.T, w_gate, w_up, w_down, partner[None, :])
    return (loss[0, 0], token_grad, gate_grad.T)


def fits_fused(mesh):
    return mesh.shape["dp"] == 4 and mesh.shape["expert"] == 8


def solution(mesh):
    placed = (
        P(("dp", "expert"), None),
        P(("dp", "expert"), None),
        P(("dp", "expert"), None),
        P("expert", "dp", None),
        P("expert", "dp", None),
        P("expert", "dp", None),
        P(),
    )
    return jax.shard_map(
        fused if fits_fused(mesh) else on_device,
        mesh=mesh,
        in_specs=placed,
        out_specs=(P(), P(("dp", "expert"), None), P(("dp", "expert"), None)),
        check_vma=False,
    )
```
